256 devices in a mesh: energy: 8 (over z), transpor: 32 (over y, x, core).
Axes of the slice: x: 4, y: 4, z: 8, core: 2. Of those that a mesh axis runs over, the one named last changes fastest.
Arguments:
- onsite: float32 [32, 2, 128, 128], P('transpor'), may hold values from -1.6 to 1.6
- coupling: float32 [32, 2, 128, 128], P('transpor'), may hold values from -0.08 to 1.2
- source_coupling: float32 [2, 128, 128], replicated, may hold values from -0.5 to 0.5
- energy: float32 [8], P('energy'), may hold values from -0.5 to 0.5
- broadening: float32 [8], P('energy'), may hold values from 0.05 to 0.2
- weights: float32 [8], P('energy'), may hold values from 0.02 to 0.08
Outputs:
- density: float32 [32, 128], P('transpor', 'energy')
The draws below stay inside these ranges and needn't reach their ends.
All inputs are finite; a program needn't handle non-finite values.
Results may differ from the reference program's by a relative error of at most 0.0003.
Values sent between devices are 32-bit elements; how exact they have to be, the bound alone decides.
No kernel may reach another device: no remote copies, remote signals or barrier semaphores. Data moves between devices by JAX's collectives and lax.ppermute only.
A program may use at most 64 MiB of HBM per device.

```python
import math
import jax
import jax.numpy as jnp
from jax import lax

ORB = 128
MODES = 128
SLABS = 32
NE = 8


def assemble(noise, diagonal):
    orbitals = diagonal.shape[1]
    identity = jnp.eye(orbitals, dtype=jnp.float32)
    off_diag = 1.0 - identity
    real_part = noise[:, 0] * off_diag + diagonal[:, :, None] * identity
    imag_part = noise[:, 1] * off_diag
    return jnp.stack([real_part, imag_part], 1)


def draw_onsite(key, part):
    key = jax.random.fold_in(key, 11)
    noise_key, diag_key = jax.random.split(key)
    noise = jnp.clip(0.015 * jax.random.normal(noise_key, (SLABS, 2, ORB, ORB), jnp.float32), -0.08, 0.08)
    diagonal = jax.random.uniform(diag_key, (SLABS, ORB), jnp.float32, -1.6, 1.6)
    return assemble(noise, diagonal)


def draw_coupling(key, part):
    key = jax.random.fold_in(key, 23)
    noise_key, diag_key = jax.random.split(key)
    noise = jnp.clip(0.012 * jax.random.normal(noise_key, (SLABS, 2, ORB, ORB), jnp.float32), -0.08, 0.08)
    diagonal = jax.random.uniform(diag_key, (SLABS, ORB), jnp.float32, 0.8, 1.2)
    return assemble(noise, diagonal)


def block_scale(rng, shape, cuts, least, top_value):
    gain, own = 1.0, jax.random.fold_in(rng, 6)
    for dim, blocks in cuts:
        heights = jnp.exp(jax.random.uniform(jax.random.fold_in(own, dim), (blocks,), jnp.float32, least / len(cuts), top_value / len(cuts)))
        gain = gain * jnp.repeat(heights, shape[dim] // blocks).reshape([-1 if axis == dim else 1 for axis in range(len(shape))])
    return gain


def bell_draw(key, extent, spread, most, kind=jnp.bfloat16):
    array = jax.random.normal(key, extent, jnp.float32) * spread
    return jnp.minimum(jnp.maximum(array, -most), most).astype(kind)


def setup_inputs(seed: int = 0) -> dict:
    key_list = jax.random.split(jax.random.key(seed), 7)
    return {
        "onsite": draw_onsite(jax.random.fold_in(key_list[6], 71), 0),
        "coupling": draw_coupling(jax.random.fold_in(key_list[6], 71), 0),
        "source_coupling": bell_draw(key_list[2], (2, ORB, MODES), ORB ** -0.5, 0.5, jnp.float32),
        "energy": jnp.clip(jax.random.uniform(key_list[3], (NE,), jnp.float32, -0.5, 0.5) * block_scale(key_list[3], (NE,), ((0, 8),), -0.4, 0.0), -0.5, 0.5),
        "broadening": jnp.clip(jnp.exp(math.log(0.2) - 1.3862944 * jax.random.uniform(key_list[4], (NE,), jnp.float32) ** block_scale(key_list[4], (NE,), ((0, 8),), -0.2, 0.2)), 0.05, 0.2),
        "weights": jnp.clip(jnp.exp(math.log(0.08) - 1.3862944 * jax.random.uniform(key_list[5], (NE,), jnp.float32) ** block_scale(key_list[5], (NE,), ((0, 8),), -0.2, 0.2)), 0.02, 0.08),
    }


def matmul(left_side, right_side):
    return jnp.dot(left_side.astype(jnp.float32), right_side.astype(jnp.float32), precision=lax.Precision.HIGHEST, preferred_element_type=jnp.float32)

def complex_mul(left_side, right_side):
    real_part = matmul(left_side[0], right_side[0]) - matmul(left_side[1], right_side[1])
    imag_part = matmul(left_side[0], right_side[1]) + matmul(left_side[1], right_side[0])
    return (real_part, imag_part)

def complex_solve(matrix, rhs_pair):
    orbitals = matrix[0].shape[0]
    embedded = jnp.concatenate([jnp.concatenate([matrix[0], -matrix[1]], 1), jnp.concatenate([matrix[1], matrix[0]], 1)], 0)
    stacked = jnp.concatenate([rhs_pair[0], rhs_pair[1]], 0)
    result = jnp.linalg.solve(embedded, stacked)
    return (result[:orbitals], result[orbitals:])

def gram_outer(real_part, imag_part):
    gram_real = matmul(real_part, real_part.T) + matmul(imag_part, imag_part.T)
    gram_imag = matmul(imag_part, real_part.T) - matmul(real_part, imag_part.T)
    return (gram_real, gram_imag)

def reference(onsite, coupling, source_coupling, energy, broadening, weights):
    identity = jnp.eye(ORB, dtype=jnp.float32)
    herm_real = 0.5 * (onsite[:, 0] + jnp.swapaxes(onsite[:, 0], 1, 2))
    herm_imag = 0.5 * (onsite[:, 1] - jnp.swapaxes(onsite[:, 1], 1, 2))
    source_gamma = gram_outer(source_coupling[0], source_coupling[1])
    drain_gamma = gram_outer(coupling[SLABS - 1, 0], coupling[SLABS - 1, 1])
    position = jnp.arange(SLABS)
    is_first = (position == 0).astype(jnp.float32)[:, None, None]
    is_last = (position == SLABS - 1).astype(jnp.float32)[:, None, None]
    gamma_real = is_first * source_gamma[0][None] + is_last * drain_gamma[0][None]
    gamma_imag = is_first * source_gamma[1][None] + is_last * drain_gamma[1][None]
    base_real = -herm_real - 0.5 * gamma_imag
    base_imag = -herm_imag + 0.5 * gamma_real
    above_real = -(1.0 - is_last) * coupling[:, 0]
    above_imag = -(1.0 - is_last) * coupling[:, 1]
    zero_block = jnp.zeros((1, ORB, ORB), jnp.float32)
    below_real = -jnp.concatenate([zero_block, jnp.swapaxes(coupling[:-1, 0], 1, 2)], 0)
    below_imag = jnp.concatenate([zero_block, jnp.swapaxes(coupling[:-1, 1], 1, 2)], 0)
    source_real = is_first * source_coupling[0][None]
    source_imag = is_first * source_coupling[1][None]

    def one_energy(point):
        level_real, level_imag = point
        diag_real = base_real + level_real * identity
        diag_imag = base_imag + level_imag * identity

        def forward(carry, slab):
            prev_prop, prev_part = carry
            diag_pair = (slab[0], slab[1])
            below_pair = (slab[2], slab[3])
            above_pair = (slab[4], slab[5])
            source_pair = (slab[6], slab[7])
            shifted = complex_mul(below_pair, prev_prop)
            reduced = (diag_pair[0] - shifted[0], diag_pair[1] - shifted[1])
            carried = complex_mul(below_pair, prev_part)
            rhs_now = (source_pair[0] - carried[0], source_pair[1] - carried[1])
            joined = (jnp.concatenate([above_pair[0], rhs_now[0]], 1), jnp.concatenate([above_pair[1], rhs_now[1]], 1))
            solved = complex_solve(reduced, joined)
            propagate = (solved[0][:, :ORB], solved[1][:, :ORB])
            particular = (solved[0][:, ORB:], solved[1][:, ORB:])
            return ((propagate, particular), (propagate, particular))
        zero_prop = (jnp.zeros((ORB, ORB), jnp.float32), jnp.zeros((ORB, ORB), jnp.float32))
        zero_part = (jnp.zeros((ORB, MODES), jnp.float32), jnp.zeros((ORB, MODES), jnp.float32))
        inputs = (diag_real, diag_imag, below_real, below_imag, above_real, above_imag, source_real, source_imag)
        unused, stored = lax.scan(forward, (zero_prop, zero_part), inputs)

        def backward(carry, slab):
            propagate, particular = slab
            product = complex_mul(propagate, carry)
            value = (particular[0] - product[0], particular[1] - product[1])
            return (value, value)
        unused_last, values = lax.scan(backward, zero_part, stored, reverse=True)
        return jnp.sum(values[0] * values[0] + values[1] * values[1], axis=2)
    densities = lax.map(one_energy, (energy, broadening))
    return jnp.sum(weights[:, None, None] * densities, axis=0)
```

```python
import jax
import jax.numpy as jnp
from jax import lax
from jax.experimental import pallas as pl
from jax.experimental.pallas import tpu as pltpu
from jax.sharding import PartitionSpec as P

F32 = jnp.float32
HIGHEST = lax.Precision.HIGHEST
ROWS = 8


def passed_along(value, axis, steps):
    count = lax.axis_size(axis)
    first, last = (max(0, -steps), min(count, count - steps))
    return lax.ppermute(value, axis, [(source, source + steps) for source in range(first, last)])


def dot(left, right):
    return jnp.dot(left, right, precision=HIGHEST, preferred_element_type=F32)


def row_of(value, k):
    return jnp.broadcast_to(value[k : k + 1, :], value.shape)


def column_of(value, j):
    return jnp.broadcast_to(value[:, j : j + 1], value.shape)


def tree_sum(terms):
    terms = list(terms)
    while len(terms) > 1:
        paired = [terms[i] + terms[i + 1] for i in range(0, len(terms) - 1, 2)]
        terms = paired + terms[len(terms) - len(terms) % 2 :]
    return terms[0]


def eliminate_panel(cols_re, cols_im, re, im, sub):
    cols_re, cols_im = list(cols_re), list(cols_im)
    scale_re = scale_im = None
    for k in range(ROWS):
        pr, pi = row_of(cols_re[k], k), row_of(cols_im[k], k)
        inv = 1.0 / (pr * pr + pi * pi)
        here = sub == k
        xr, xi = jnp.where(here, 0.0, cols_re[k]), jnp.where(here, 0.0, cols_im[k])
        tr, ti = xr * pr + xi * pi, xi * pr - xr * pi
        ur, ui = tr * inv, ti * inv
        for j in range(k + 1, ROWS):
            ar, ai = row_of(cols_re[j], k), row_of(cols_im[j], k)
            if j == k + 1:
                cols_re[j] = cols_re[j] - inv * (tr * ar - ti * ai)
                cols_im[j] = cols_im[j] - inv * (tr * ai + ti * ar)
            else:
                cols_re[j] = cols_re[j] - (ur * ar - ui * ai)
                cols_im[j] = cols_im[j] - (ur * ai + ui * ar)
        ar, ai = row_of(re, k), row_of(im, k)
        re, im = re - (ur * ar - ui * ai), im - (ur * ai + ui * ar)
        qr, qi = pr * inv, -(pi * inv)
        scale_re = qr if k == 0 else jnp.where(here, qr, scale_re)
        scale_im = qi if k == 0 else jnp.where(here, qi, scale_im)
    return re * scale_re - im * scale_im, re * scale_im + im * scale_re


def inverse(re, im):
    size = re.shape[0]
    count = size // ROWS
    a = [re[ROWS * b : ROWS * (b + 1)] for b in range(count)]
    c = [im[ROWS * b : ROWS * (b + 1)] for b in range(count)]
    sub = lax.broadcasted_iota(jnp.int32, (ROWS, size), 0)
    lane = lax.broadcasted_iota(jnp.int32, (ROWS, size), 1)
    zeros = jnp.zeros((ROWS, 2 * size), F32)
    for t in range(count):
        base = ROWS * t
        pivots = (lane >= base) & (lane < base + ROWS)
        unit = (lane - base == sub).astype(F32)
        cols_re = [column_of(a[t], base + j) for j in range(ROWS)]
        cols_im = [column_of(c[t], base + j) for j in range(ROWS)]
        row_re, row_im = eliminate_panel(
            cols_re, cols_im, jnp.where(pivots, unit, a[t]), jnp.where(pivots, 0.0, c[t]), sub
        )
        ahead = t + 1
        if ahead < count:
            mr = [column_of(a[ahead], base + j) for j in range(ROWS)]
            mi = [column_of(c[ahead], base + j) for j in range(ROWS)]
            br = [row_of(row_re, j) for j in range(ROWS)]
            bi = [row_of(row_im, j) for j in range(ROWS)]
            tr = tree_sum(mr[j] * br[j] - mi[j] * bi[j] for j in range(ROWS))
            ti = tree_sum(mr[j] * bi[j] + mi[j] * br[j] for j in range(ROWS))
            ahead_re = jnp.where(pivots, 0.0, a[ahead]) - tr
            ahead_im = jnp.where(pivots, 0.0, c[ahead]) - ti
        others = [b for b in range(count) if b not in (t, ahead)]
        left = jnp.concatenate(
            [
                jnp.concatenate([a[b] for b in others], 0),
                jnp.concatenate([c[b] for b in others], 0),
            ],
            1,
        )
        top = jnp.concatenate([row_re, row_im], 1)
        low = jnp.concatenate([-row_im, row_re], 1)
        right = [zeros] * t + [top] + [zeros] * (count - 1) + [low] + [zeros] * (count - 1 - t)
        change = dot(left, jnp.concatenate(right, 0))
        for x, b in enumerate(others):
            rows = slice(ROWS * x, ROWS * (x + 1))
            a[b] = jnp.where(pivots, 0.0, a[b]) - change[rows, :size]
            c[b] = jnp.where(pivots, 0.0, c[b]) - change[rows, size:]
        a[t], c[t] = row_re, row_im
        if ahead < count:
            a[ahead], c[ahead] = ahead_re, ahead_im
    return jnp.concatenate(a, 0), jnp.concatenate(c, 0)


def stacked(re, im):
    return jnp.concatenate(
        [jnp.concatenate([re, im], 1), jnp.concatenate([-im, re], 1)], 0
    )


def times(left_re, left_im, right_re, right_im):
    return dot(jnp.concatenate([left_re, left_im], 1), stacked(right_re, right_im))


def vmem(count):
    return [pl.BlockSpec(memory_space=pltpu.VMEM)] * count


SMEM = pl.BlockSpec(memory_space=pltpu.SMEM)


def first_kernel(place_ref, point_ref, onsite_ref, coupling_ref, source_ref, diag_ref, inv_ref):
    size = onsite_ref.shape[-1]
    place, last = place_ref[0], place_ref[1]
    is_first, is_last = place == 0, place == last
    kr = jnp.where(is_first, source_ref[0], jnp.where(is_last, coupling_ref[0, 0], 0.0))
    ki = jnp.where(is_first, source_ref[1], jnp.where(is_last, coupling_ref[0, 1], 0.0))
    krt, kit = kr.T, ki.T
    gamma = times(kr, ki, krt, -kit)
    re, im = onsite_ref[0, 0], onsite_ref[0, 1]
    row = lax.broadcasted_iota(jnp.int32, (size, size), 0)
    col = lax.broadcasted_iota(jnp.int32, (size, size), 1)
    unit = (row == col).astype(F32)
    diag_re = point_ref[0] * unit - 0.5 * (re + re.T) - 0.5 * gamma[:, size:]
    diag_im = point_ref[1] * unit - 0.5 * (im - im.T) + 0.5 * gamma[:, :size]
    diag_ref[0], diag_ref[1] = diag_re, diag_im
    inv_ref[0], inv_ref[1] = inverse(diag_re, diag_im)


def solve_into(inv_ref, left_re, left_im, right_re, right_im, yl_ref, yu_ref):
    size = left_re.shape[-1]
    ir, ii = inv_ref[0], inv_ref[1]
    yl = times(ir, ii, left_re, left_im)
    yl_ref[0], yl_ref[1] = yl[:, :size], yl[:, size:]
    yu = times(ir, ii, right_re, right_im)
    yu_ref[0], yu_ref[1] = yu[:, :size], yu[:, size:]


def start_kernel(
    place_ref, inv_ref, behind_ref, coupling_ref, source_ref, yl_ref, yu_ref, left_ref, right_ref
):
    place, last = place_ref[0], place_ref[1]
    left_re = jnp.where(place == 0, source_ref[0], -behind_ref[0, 0].T)
    left_im = jnp.where(place == 0, source_ref[1], behind_ref[0, 1].T)
    right_re = jnp.where(place == last, 0.0, -coupling_ref[0, 0])
    right_im = jnp.where(place == last, 0.0, -coupling_ref[0, 1])
    left_ref[0], left_ref[1] = left_re, left_im
    right_ref[0], right_ref[1] = right_re, right_im
    solve_into(inv_ref, left_re, left_im, right_re, right_im, yl_ref, yu_ref)


def invert_kernel(diag_ref, left_ref, right_ref, from_left_ref, from_right_ref, out_ref, inv_ref):
    size = diag_ref.shape[-1]
    lr, li, rr, ri = left_ref[0], left_ref[1], right_ref[0], right_ref[1]
    change = times(lr, li, from_left_ref[0], from_left_ref[1]) + times(
        rr, ri, from_right_ref[0], from_right_ref[1]
    )
    re = diag_ref[0] - change[:, :size]
    im = diag_ref[1] - change[:, size:]
    out_ref[0], out_ref[1] = re, im
    inv_ref[0], inv_ref[1] = inverse(re, im)


def next_left(keep, left_ref, from_left_ref):
    size = left_ref.shape[-1]
    made = times(left_ref[0], left_ref[1], from_left_ref[0], from_left_ref[1])
    return (
        jnp.where(keep, left_ref[0], -made[:, :size]),
        jnp.where(keep, left_ref[1], -made[:, size:]),
    )


def step_kernel(
    keep_ref,
    inv_ref,
    left_ref,
    right_ref,
    from_left_ref,
    from_right_ref,
    yl_ref,
    yu_ref,
    left_out_ref,
    right_out_ref,
):
    size = left_ref.shape[-1]
    left_re, left_im = next_left(keep_ref[0] == 1, left_ref, from_left_ref)
    made = times(right_ref[0], right_ref[1], from_right_ref[0], from_right_ref[1])
    right_re, right_im = -made[:, :size], -made[:, size:]
    left_out_ref[0], left_out_ref[1] = left_re, left_im
    right_out_ref[0], right_out_ref[1] = right_re, right_im
    solve_into(inv_ref, left_re, left_im, right_re, right_im, yl_ref, yu_ref)


def last_kernel(keep_ref, weight_ref, inv_ref, left_ref, from_left_ref, out_ref):
    size = left_ref.shape[-1]
    rhs_re, rhs_im = next_left(keep_ref[0] == 1, left_ref, from_left_ref)
    x = times(inv_ref[0], inv_ref[1], rhs_re, rhs_im)
    square = x * x
    both = square[:, :size] + square[:, size:]
    total = lax.dot_general(
        jnp.ones((8, size), F32),
        both,
        (((1,), (1,)), ((), ())),
        precision=HIGHEST,
        preferred_element_type=F32,
    )
    out_ref[...] = total * weight_ref[0]


def call(kernel, outs, specs, flops=0):
    return pl.pallas_call(
        kernel,
        out_shape=outs,
        in_specs=specs,
        out_specs=jax.tree.map(lambda _: pl.BlockSpec(memory_space=pltpu.VMEM), outs),
        compiler_params=pltpu.CompilerParams(vmem_limit_bytes=16 << 20),
        cost_estimate=pl.CostEstimate(flops=flops, bytes_accessed=1 << 20, transcendentals=0),
    )


def summed_over(value, axis):
    count = lax.axis_size(axis)
    me = lax.axis_index(axis)
    total = lax.dynamic_slice_in_dim(value, me, 1, 0)
    for shift in range(1, count):
        pairs = [(s, (s + shift) % count) for s in range(count)]
        part = lax.dynamic_slice_in_dim(value, (me + shift) % count, 1, 0)
        total = total + lax.ppermute(part, axis, pairs)
    return total


def local(onsite, coupling, source_coupling, energy, broadening, weights):
    size = onsite.shape[2]
    devices = lax.axis_size("transpor")
    position = lax.axis_index("transpor")
    levels = devices.bit_length() - 1
    block = jax.ShapeDtypeStruct((2, size, size), F32)
    place = jnp.stack([position, jnp.int32(devices - 1)]).astype(jnp.int32)
    point = jnp.concatenate([energy, broadening])
    behind = passed_along(coupling, "transpor", 1)
    diag, inv = call(first_kernel, [block] * 2, [SMEM, SMEM] + vmem(3), 4 << 30)(
        place, point, onsite, coupling, source_coupling
    )
    yl, yu, left, right = call(start_kernel, [block] * 4, [SMEM] + vmem(4))(
        place, inv, behind, coupling, source_coupling
    )
    for level in range(levels):
        distance = 1 << level
        yu_from_left = passed_along(yu, "transpor", distance)
        yl_from_right = passed_along(yl, "transpor", -distance)
        yl_from_left = passed_along(yl, "transpor", distance)
        diag, inv = call(invert_kernel, [block] * 2, vmem(5), 4 << 30)(
            diag, left, right, yu_from_left, yl_from_right
        )
        keep = (position < distance).astype(jnp.int32)[None]
        if level < levels - 1:
            yu_from_right = passed_along(yu, "transpor", -distance)
            yl, yu, left, right = call(step_kernel, [block] * 4, [SMEM] + vmem(5))(
                keep, inv, left, right, yl_from_left, yu_from_right
            )
    count = lax.axis_size("energy")
    row = call(last_kernel, jax.ShapeDtypeStruct((8, size), F32), [SMEM, SMEM] + vmem(3))(
        keep, weights, inv, left, yl_from_left
    )
    return summed_over(row[0].reshape(count, size // count), "energy")


def solution(mesh):
    placed = (
        P("transpor", None, None, None),
        P("transpor", None, None, None),
        P(),
        P("energy"),
        P("energy"),
        P("energy"),
    )
    return jax.shard_map(
        local, mesh=mesh, in_specs=placed, out_specs=P("transpor", "energy"), check_vma=False
    )
```

```python
import jax
import jax.numpy as jnp
from jax import lax
from jax.experimental import pallas as pl
from jax.experimental.pallas import tpu as pltpu
from jax.sharding import PartitionSpec as P

F32 = jnp.float32
HIGHEST = lax.Precision.HIGHEST
ROWS = 8


def dot(left, right):
    return jnp.dot(left, right, precision=HIGHEST, preferred_element_type=F32)


def row_of(value, k):
    return jnp.broadcast_to(value[k : k + 1, :], value.shape)


def column_of(value, j):
    return jnp.broadcast_to(value[:, j : j + 1], value.shape)


def tree_sum(terms):
    terms = list(terms)
    while len(terms) > 1:
        paired = [terms[i] + terms[i + 1] for i in range(0, len(terms) - 1, 2)]
        terms = paired + terms[len(terms) - len(terms) % 2 :]
    return terms[0]


def eliminate_panel(cols_re, cols_im, re, im, sub):
    cols_re, cols_im = list(cols_re), list(cols_im)
    scale_re = scale_im = None
    for k in range(ROWS):
        pr, pi = row_of(cols_re[k], k), row_of(cols_im[k], k)
        inv = 1.0 / (pr * pr + pi * pi)
        here = sub == k
        xr, xi = jnp.where(here, 0.0, cols_re[k]), jnp.where(here, 0.0, cols_im[k])
        tr, ti = xr * pr + xi * pi, xi * pr - xr * pi
        ur, ui = tr * inv, ti * inv
        for j in range(k + 1, ROWS):
            ar, ai = row_of(cols_re[j], k), row_of(cols_im[j], k)
            if j == k + 1:
                cols_re[j] = cols_re[j] - inv * (tr * ar - ti * ai)
                cols_im[j] = cols_im[j] - inv * (tr * ai + ti * ar)
            else:
                cols_re[j] = cols_re[j] - (ur * ar - ui * ai)
                cols_im[j] = cols_im[j] - (ur * ai + ui * ar)
        ar, ai = row_of(re, k), row_of(im, k)
        re, im = re - (ur * ar - ui * ai), im - (ur * ai + ui * ar)
        qr, qi = pr * inv, -(pi * inv)
        scale_re = qr if k == 0 else jnp.where(here, qr, scale_re)
        scale_im = qi if k == 0 else jnp.where(here, qi, scale_im)
    return re * scale_re - im * scale_im, re * scale_im + im * scale_re


def inverse(re, im):
    size = re.shape[0]
    count = size // ROWS
    a = [re[ROWS * b : ROWS * (b + 1)] for b in range(count)]
    c = [im[ROWS * b : ROWS * (b + 1)] for b in range(count)]
    sub = lax.broadcasted_iota(jnp.int32, (ROWS, size), 0)
    lane = lax.broadcasted_iota(jnp.int32, (ROWS, size), 1)
    zeros = jnp.zeros((ROWS, 2 * size), F32)
    for t in range(count):
        base = ROWS * t
        pivots = (lane >= base) & (lane < base + ROWS)
        unit = (lane - base == sub).astype(F32)
        cols_re = [column_of(a[t], base + j) for j in range(ROWS)]
        cols_im = [column_of(c[t], base + j) for j in range(ROWS)]
        row_re, row_im = eliminate_panel(
            cols_re, cols_im, jnp.where(pivots, unit, a[t]), jnp.where(pivots, 0.0, c[t]), sub
        )
        ahead = t + 1
        if ahead < count:
            mr = [column_of(a[ahead], base + j) for j in range(ROWS)]
            mi = [column_of(c[ahead], base + j) for j in range(ROWS)]
            br = [row_of(row_re, j) for j in range(ROWS)]
            bi = [row_of(row_im, j) for j in range(ROWS)]
            tr = tree_sum(mr[j] * br[j] - mi[j] * bi[j] for j in range(ROWS))
            ti = tree_sum(mr[j] * bi[j] + mi[j] * br[j] for j in range(ROWS))
            ahead_re = jnp.where(pivots, 0.0, a[ahead]) - tr
            ahead_im = jnp.where(pivots, 0.0, c[ahead]) - ti
        others = [b for b in range(count) if b not in (t, ahead)]
        left = jnp.concatenate(
            [
                jnp.concatenate([a[b] for b in others], 0),
                jnp.concatenate([c[b] for b in others], 0),
            ],
            1,
        )
        top = jnp.concatenate([row_re, row_im], 1)
        low = jnp.concatenate([-row_im, row_re], 1)
        right = [zeros] * t + [top] + [zeros] * (count - 1) + [low] + [zeros] * (count - 1 - t)
        change = dot(left, jnp.concatenate(right, 0))
        for x, b in enumerate(others):
            rows = slice(ROWS * x, ROWS * (x + 1))
            a[b] = jnp.where(pivots, 0.0, a[b]) - change[rows, :size]
            c[b] = jnp.where(pivots, 0.0, c[b]) - change[rows, size:]
        a[t], c[t] = row_re, row_im
        if ahead < count:
            a[ahead], c[ahead] = ahead_re, ahead_im
    return jnp.concatenate(a, 0), jnp.concatenate(c, 0)


def stacked(re, im):
    return jnp.concatenate(
        [jnp.concatenate([re, im], 1), jnp.concatenate([-im, re], 1)], 0
    )


def times(left_re, left_im, right_re, right_im):
    return dot(jnp.concatenate([left_re, left_im], 1), stacked(right_re, right_im))


def vmem(count):
    return [pl.BlockSpec(memory_space=pltpu.VMEM)] * count


SMEM = pl.BlockSpec(memory_space=pltpu.SMEM)


def first_kernel(
    place_ref,
    point_ref,
    onsite_any,
    coupling_any,
    source_any,
    diag_ref,
    inv_ref,
    onsite_ref,
    coupling_ref,
    source_ref,
    sems,
):
    copies = [
        pltpu.make_async_copy(onsite_any, onsite_ref, sems.at[0]),
        pltpu.make_async_copy(coupling_any, coupling_ref, sems.at[1]),
        pltpu.make_async_copy(source_any, source_ref, sems.at[2]),
    ]
    for copy in copies:
        copy.start()
    for copy in copies:
        copy.wait()
    size = onsite_ref.shape[-1]
    place, last = place_ref[0], place_ref[1]
    is_first, is_last = place == 0, place == last
    kr = jnp.where(is_first, source_ref[0], jnp.where(is_last, coupling_ref[0, 0], 0.0))
    ki = jnp.where(is_first, source_ref[1], jnp.where(is_last, coupling_ref[0, 1], 0.0))
    krt, kit = kr.T, ki.T
    gamma = times(kr, ki, krt, -kit)
    re, im = onsite_ref[0, 0], onsite_ref[0, 1]
    row = lax.broadcasted_iota(jnp.int32, (size, size), 0)
    col = lax.broadcasted_iota(jnp.int32, (size, size), 1)
    unit = (row == col).astype(F32)
    diag_re = point_ref[0] * unit - 0.5 * (re + re.T) - 0.5 * gamma[:, size:]
    diag_im = point_ref[1] * unit - 0.5 * (im - im.T) + 0.5 * gamma[:, :size]
    diag_ref[0], diag_ref[1] = diag_re, diag_im
    inv_ref[0], inv_ref[1] = inverse(diag_re, diag_im)


def solve_into(inv_re, inv_im, left_re, left_im, right_re, right_im, solved_ref):
    size = left_re.shape[-1]
    left = times(inv_re, inv_im, left_re, left_im)
    solved_ref[0], solved_ref[1] = left[:, :size], left[:, size:]
    right = times(inv_re, inv_im, right_re, right_im)
    solved_ref[2], solved_ref[3] = right[:, :size], right[:, size:]


def start_kernel(
    place_ref, inv_ref, behind_ref, coupling_ref, source_ref, solved_ref, left_ref, right_ref
):
    place, last = place_ref[0], place_ref[1]
    left_re = jnp.where(place == 0, source_ref[0], -behind_ref[0, 0].T)
    left_im = jnp.where(place == 0, source_ref[1], behind_ref[0, 1].T)
    right_re = jnp.where(place == last, 0.0, -coupling_ref[0, 0])
    right_im = jnp.where(place == last, 0.0, -coupling_ref[0, 1])
    left_ref[0], left_ref[1] = left_re, left_im
    right_ref[0], right_ref[1] = right_re, right_im
    solve_into(inv_ref[0], inv_ref[1], left_re, left_im, right_re, right_im, solved_ref)


def neighbours(flag_ref, near_ref, far_ref):
    swapped = flag_ref[1] == 1
    has_left = flag_ref[0] == 1
    left = [
        jnp.where(has_left, jnp.where(swapped, near_ref[k], far_ref[k]), 0.0) for k in range(4)
    ]
    right = [jnp.where(swapped, far_ref[k], near_ref[k]) for k in range(4)]
    return left, right


def level_kernel(
    flag_ref,
    diag_ref,
    left_ref,
    right_ref,
    near_ref,
    far_ref,
    solved_ref,
    diag_out_ref,
    left_out_ref,
    right_out_ref,
):
    size = diag_ref.shape[-1]
    has_left = flag_ref[0] == 1
    from_left, from_right = neighbours(flag_ref, near_ref, far_ref)
    change = times(left_ref[0], left_ref[1], from_left[2], from_left[3]) + times(
        right_ref[0], right_ref[1], from_right[0], from_right[1]
    )
    re, im = diag_ref[0] - change[:, :size], diag_ref[1] - change[:, size:]
    diag_out_ref[0], diag_out_ref[1] = re, im
    made = times(left_ref[0], left_ref[1], from_left[0], from_left[1])
    left_re = jnp.where(has_left, -made[:, :size], left_ref[0])
    left_im = jnp.where(has_left, -made[:, size:], left_ref[1])
    made = times(right_ref[0], right_ref[1], from_right[2], from_right[3])
    right_re, right_im = -made[:, :size], -made[:, size:]
    left_out_ref[0], left_out_ref[1] = left_re, left_im
    right_out_ref[0], right_out_ref[1] = right_re, right_im
    inv_re, inv_im = inverse(re, im)
    solve_into(inv_re, inv_im, left_re, left_im, right_re, right_im, solved_ref)


def last_kernel(flag_ref, weight_ref, diag_ref, left_ref, right_ref, near_ref, out_ref):
    size = diag_ref.shape[-1]
    has_left = flag_ref[0] == 1
    link_re = jnp.where(has_left, left_ref[0], right_ref[0])
    link_im = jnp.where(has_left, left_ref[1], right_ref[1])
    change = times(
        link_re,
        link_im,
        jnp.where(has_left, near_ref[2], near_ref[0]),
        jnp.where(has_left, near_ref[3], near_ref[1]),
    )
    made = times(left_ref[0], left_ref[1], near_ref[0], near_ref[1])
    rhs_re = jnp.where(has_left, -made[:, :size], left_ref[0])
    rhs_im = jnp.where(has_left, -made[:, size:], left_ref[1])
    inv_re, inv_im = inverse(diag_ref[0] - change[:, :size], diag_ref[1] - change[:, size:])
    x = times(inv_re, inv_im, rhs_re, rhs_im)
    square = x * x
    both = square[:, :size] + square[:, size:]
    total = lax.dot_general(
        jnp.ones((8, size), F32),
        both,
        (((1,), (1,)), ((), ())),
        precision=HIGHEST,
        preferred_element_type=F32,
    )
    out_ref[...] = total * weight_ref[0]


def call(kernel, outs, specs, flops=0, scratch=(), limit=16 << 20):
    return pl.pallas_call(
        kernel,
        scratch_shapes=list(scratch),
        out_shape=outs,
        in_specs=specs,
        out_specs=jax.tree.map(lambda _: pl.BlockSpec(memory_space=pltpu.VMEM), outs),
        compiler_params=pltpu.CompilerParams(vmem_limit_bytes=limit),
        cost_estimate=pl.CostEstimate(flops=flops, bytes_accessed=1 << 20, transcendentals=0),
    )


def summed_over(value, axis):
    parts = lax.all_to_all(value, axis, 0, 0, tiled=True)
    return jnp.sum(parts, axis=0, keepdims=True)


def local(onsite, coupling, source_coupling, energy, broadening, weights):
    size = onsite.shape[2]
    devices = lax.axis_size("transpor")
    position = lax.axis_index("transpor")
    levels = devices.bit_length() - 1
    block = jax.ShapeDtypeStruct((2, size, size), F32)
    pair = jax.ShapeDtypeStruct((4, size, size), F32)
    place = jnp.stack([position, jnp.int32(devices - 1)]).astype(jnp.int32)
    point = jnp.concatenate([energy, broadening])
    behind = lax.ppermute(
        coupling, "transpor", [(s, (s + 1) % devices) for s in range(devices)]
    )
    scratch = [
        pltpu.VMEM(onsite.shape, F32),
        pltpu.VMEM(coupling.shape, F32),
        pltpu.VMEM(source_coupling.shape, F32),
        pltpu.SemaphoreType.DMA((3,)),
    ]
    anywhere = [pl.BlockSpec(memory_space=pl.ANY)] * 3
    diag, inv = call(
        first_kernel, [block] * 2, [SMEM, SMEM] + anywhere, 4 << 30, scratch, 60 << 20
    )(place, point, onsite, coupling, source_coupling)
    solved, left, right = call(start_kernel, [pair, block, block], [SMEM] + vmem(4))(
        place, inv, behind, coupling, source_coupling
    )
    for level in range(levels):
        distance = 1 << level
        swapped = (position >> level) & 1
        flags = jnp.stack([(position >= distance).astype(jnp.int32), swapped])
        near = lax.ppermute(solved, "transpor", [(s, s ^ distance) for s in range(devices)])
        if level < levels - 1:
            far = lax.ppermute(
                solved,
                "transpor",
                [
                    (s, (s + (distance if s & distance else -distance)) % devices)
                    for s in range(devices)
                ],
            )
            solved, diag, left, right = call(
                level_kernel, [pair, block, block, block], [SMEM] + vmem(5), 4 << 30
            )(flags, diag, left, right, near, far)
    count = lax.axis_size("energy")
    row = call(last_kernel, jax.ShapeDtypeStruct((8, size), F32), [SMEM, SMEM] + vmem(4))(
        flags, weights, diag, left, right, near
    )
    return summed_over(row[0].reshape(count, size // count), "energy")


def solution(mesh):
    placed = (
        P("transpor", None, None, None),
        P("transpor", None, None, None),
        P(),
        P("energy"),
        P("energy"),
        P("energy"),
    )
    return jax.shard_map(
        local, mesh=mesh, in_specs=placed, out_specs=P("transpor", "energy"), check_vma=False
    )
```

```python
import functools

import jax
import jax.numpy as jnp
from jax import lax
from jax.experimental import pallas as pl
from jax.experimental.pallas import tpu as pltpu
from jax.sharding import PartitionSpec as P

F32 = jnp.float32
HIGHEST = lax.Precision.HIGHEST
ROWS = 8
SPLIT_LEVELS = (0, 1, 2, 3, 4)


def dot(left, right):
    return jnp.dot(left, right, precision=HIGHEST, preferred_element_type=F32)


def row_of(value, k):
    return jnp.broadcast_to(value[k : k + 1, :], value.shape)


def column_of(value, j):
    return jnp.broadcast_to(value[:, j : j + 1], value.shape)


def tree_sum(terms):
    terms = list(terms)
    while len(terms) > 1:
        paired = [terms[i] + terms[i + 1] for i in range(0, len(terms) - 1, 2)]
        terms = paired + terms[len(terms) - len(terms) % 2 :]
    return terms[0]


def eliminate_panel(cols_re, cols_im, re, im, sub):
    cols_re, cols_im = list(cols_re), list(cols_im)
    scale_re = scale_im = None
    for k in range(ROWS):
        pr, pi = row_of(cols_re[k], k), row_of(cols_im[k], k)
        inv = 1.0 / (pr * pr + pi * pi)
        here = sub == k
        xr, xi = jnp.where(here, 0.0, cols_re[k]), jnp.where(here, 0.0, cols_im[k])
        tr, ti = xr * pr + xi * pi, xi * pr - xr * pi
        ur, ui = tr * inv, ti * inv
        for j in range(k + 1, ROWS):
            ar, ai = row_of(cols_re[j], k), row_of(cols_im[j], k)
            if j == k + 1:
                cols_re[j] = cols_re[j] - inv * (tr * ar - ti * ai)
                cols_im[j] = cols_im[j] - inv * (tr * ai + ti * ar)
            else:
                cols_re[j] = cols_re[j] - (ur * ar - ui * ai)
                cols_im[j] = cols_im[j] - (ur * ai + ui * ar)
        ar, ai = row_of(re, k), row_of(im, k)
        re, im = re - (ur * ar - ui * ai), im - (ur * ai + ui * ar)
        qr, qi = pr * inv, -(pi * inv)
        scale_re = qr if k == 0 else jnp.where(here, qr, scale_re)
        scale_im = qi if k == 0 else jnp.where(here, qi, scale_im)
    return re * scale_re - im * scale_im, re * scale_im + im * scale_re


def inverse(re, im):
    size = re.shape[0]
    count = size // ROWS
    a = [re[ROWS * b : ROWS * (b + 1)] for b in range(count)]
    c = [im[ROWS * b : ROWS * (b + 1)] for b in range(count)]
    sub = lax.broadcasted_iota(jnp.int32, (ROWS, size), 0)
    lane = lax.broadcasted_iota(jnp.int32, (ROWS, size), 1)
    zeros = jnp.zeros((ROWS, 2 * size), F32)
    for t in range(count):
        base = ROWS * t
        pivots = (lane >= base) & (lane < base + ROWS)
        unit = (lane - base == sub).astype(F32)
        cols_re = [column_of(a[t], base + j) for j in range(ROWS)]
        cols_im = [column_of(c[t], base + j) for j in range(ROWS)]
        row_re, row_im = eliminate_panel(
            cols_re, cols_im, jnp.where(pivots, unit, a[t]), jnp.where(pivots, 0.0, c[t]), sub
        )
        ahead = t + 1
        if ahead < count:
            mr = [column_of(a[ahead], base + j) for j in range(ROWS)]
            mi = [column_of(c[ahead], base + j) for j in range(ROWS)]
            br = [row_of(row_re, j) for j in range(ROWS)]
            bi = [row_of(row_im, j) for j in range(ROWS)]
            tr = tree_sum(mr[j] * br[j] - mi[j] * bi[j] for j in range(ROWS))
            ti = tree_sum(mr[j] * bi[j] + mi[j] * br[j] for j in range(ROWS))
            ahead_re = jnp.where(pivots, 0.0, a[ahead]) - tr
            ahead_im = jnp.where(pivots, 0.0, c[ahead]) - ti
        others = [b for b in range(count) if b not in (t, ahead)]
        left = jnp.concatenate(
            [
                jnp.concatenate([a[b] for b in others], 0),
                jnp.concatenate([c[b] for b in others], 0),
            ],
            1,
        )
        top = jnp.concatenate([row_re, row_im], 1)
        low = jnp.concatenate([-row_im, row_re], 1)
        right = [zeros] * t + [top] + [zeros] * (count - 1) + [low] + [zeros] * (count - 1 - t)
        change = dot(left, jnp.concatenate(right, 0))
        for x, b in enumerate(others):
            rows = slice(ROWS * x, ROWS * (x + 1))
            a[b] = jnp.where(pivots, 0.0, a[b]) - change[rows, :size]
            c[b] = jnp.where(pivots, 0.0, c[b]) - change[rows, size:]
        a[t], c[t] = row_re, row_im
        if ahead < count:
            a[ahead], c[ahead] = ahead_re, ahead_im
    return jnp.concatenate(a, 0), jnp.concatenate(c, 0)


def stacked(re, im):
    return jnp.concatenate(
        [jnp.concatenate([re, im], 1), jnp.concatenate([-im, re], 1)], 0
    )


def times(left_re, left_im, right_re, right_im):
    return dot(jnp.concatenate([left_re, left_im], 1), stacked(right_re, right_im))


def vmem(count):
    return [pl.BlockSpec(memory_space=pltpu.VMEM)] * count


SMEM = pl.BlockSpec(memory_space=pltpu.SMEM)


def first_kernel(energy_ref, broadening_ref, onsite_ref, contact_ref, diag_ref, inv_ref):
    size = onsite_ref.shape[-1]
    re, im, kr, ki = onsite_ref[0, 0], onsite_ref[0, 1], contact_ref[0], contact_ref[1]
    krt, kit = kr.T, ki.T
    gamma = times(kr, ki, krt, -kit)
    row = lax.broadcasted_iota(jnp.int32, (size, size), 0)
    col = lax.broadcasted_iota(jnp.int32, (size, size), 1)
    unit = (row == col).astype(F32)
    diag_re = energy_ref[0] * unit - 0.5 * (re + re.T) - 0.5 * gamma[:, size:]
    diag_im = broadening_ref[0] * unit - 0.5 * (im - im.T) + 0.5 * gamma[:, :size]
    diag_ref[0], diag_ref[1] = diag_re, diag_im
    inv_ref[0], inv_ref[1] = inverse(diag_re, diag_im)


def is_odd(level):
    return ((lax.axis_index("transpor") >> level) & 1) == 1


def solve_into(inv_re, inv_im, left_re, left_im, right_re, right_im, solved_refs, level):
    size = left_re.shape[-1]
    left = times(inv_re, inv_im, left_re, left_im)
    right = times(inv_re, inv_im, right_re, right_im)
    if len(solved_refs) == 1:
        (solved_ref,) = solved_refs
        solved_ref[0], solved_ref[1] = left[:, :size], left[:, size:]
        solved_ref[2], solved_ref[3] = right[:, :size], right[:, size:]
    else:
        odd = is_odd(level)
        early, late = jnp.where(odd, left, right), jnp.where(odd, right, left)
        for ref, value in zip(solved_refs, (early, late)):
            ref[0], ref[1] = value[:, :size], value[:, size:]


def start_kernel(inv_ref, behind_ref, coupling_ref, source_ref, left_ref, right_ref, *solved_refs):
    place, count = lax.axis_index("transpor"), lax.axis_size("transpor")
    left_re = jnp.where(place == 0, source_ref[0], -behind_ref[0, 0].T)
    left_im = jnp.where(place == 0, source_ref[1], behind_ref[0, 1].T)
    right_re = jnp.where(place == count - 1, 0.0, -coupling_ref[0, 0])
    right_im = jnp.where(place == count - 1, 0.0, -coupling_ref[0, 1])
    left_ref[0], left_ref[1] = left_re, left_im
    right_ref[0], right_ref[1] = right_re, right_im
    solve_into(inv_ref[0], inv_ref[1], left_re, left_im, right_re, right_im, solved_refs, 0)


def has_left(level):
    return lax.axis_index("transpor") >= (1 << level)


def either(odd, one, other):
    return [jnp.where(odd, one[k], other[k]) for k in range(2)]


def reduced_diag(level, diag_ref, left_ref, right_ref, across_left, across_right):
    size = diag_ref.shape[-1]
    across_left = [jnp.where(has_left(level), part, 0.0) for part in across_left]
    change = times(left_ref[0], left_ref[1], *across_left) + times(
        right_ref[0], right_ref[1], *across_right
    )
    return diag_ref[0] - change[:, :size], diag_ref[1] - change[:, size:]


def next_couplings(level, left_ref, right_ref, beyond_left, beyond_right):
    size = left_ref.shape[-1]
    made = times(left_ref[0], left_ref[1], *beyond_left)
    left_re = jnp.where(has_left(level), -made[:, :size], left_ref[0])
    left_im = jnp.where(has_left(level), -made[:, size:], left_ref[1])
    made = times(right_ref[0], right_ref[1], *beyond_right)
    return left_re, left_im, -made[:, :size], -made[:, size:]


def level_kernel(
    level,
    diag_ref,
    left_ref,
    right_ref,
    near_ref,
    far_ref,
    diag_out_ref,
    left_out_ref,
    right_out_ref,
    *solved_refs,
):
    odd = is_odd(level)
    near, far = near_ref, far_ref
    across_left = either(odd, near[2:], far[2:])
    across_right = either(odd, far[:2], near[:2])
    re, im = reduced_diag(level, diag_ref, left_ref, right_ref, across_left, across_right)
    diag_out_ref[0], diag_out_ref[1] = re, im
    beyond_left = either(odd, near[:2], far[:2])
    beyond_right = either(odd, far[2:], near[2:])
    blocks = next_couplings(level, left_ref, right_ref, beyond_left, beyond_right)
    left_out_ref[0], left_out_ref[1], right_out_ref[0], right_out_ref[1] = blocks
    inv_re, inv_im = inverse(re, im)
    solve_into(inv_re, inv_im, *blocks, solved_refs, level + 1)


def invert_kernel(
    level, diag_ref, left_ref, right_ref, near_ref, far_ref, diag_out_ref, inv_ref
):
    odd = is_odd(level)
    across_left = either(odd, near_ref, far_ref)
    across_right = either(odd, far_ref, near_ref)
    re, im = reduced_diag(level, diag_ref, left_ref, right_ref, across_left, across_right)
    diag_out_ref[0], diag_out_ref[1] = re, im
    inv_ref[0], inv_ref[1] = inverse(re, im)


def couple_kernel(
    level,
    inv_ref,
    left_ref,
    right_ref,
    near_ref,
    far_ref,
    left_out_ref,
    right_out_ref,
    *solved_refs,
):
    odd = is_odd(level)
    beyond_left = either(odd, near_ref, far_ref)
    beyond_right = either(odd, far_ref, near_ref)
    blocks = next_couplings(level, left_ref, right_ref, beyond_left, beyond_right)
    left_out_ref[0], left_out_ref[1], right_out_ref[0], right_out_ref[1] = blocks
    solve_into(inv_ref[0], inv_ref[1], *blocks, solved_refs, level + 1)


def link_change(level, left_ref, right_ref, near_ref):
    reached = has_left(level)
    link = [jnp.where(reached, left_ref[k], right_ref[k]) for k in range(2)]
    if near_ref.shape[0] == 2:
        return times(*link, near_ref[0], near_ref[1])
    return times(*link, *(jnp.where(reached, near_ref[k + 2], near_ref[k]) for k in range(2)))


def finish(level, weight_ref, inv_re, inv_im, left_ref, near_ref, out_ref):
    size = left_ref.shape[-1]
    made = times(left_ref[0], left_ref[1], near_ref[0], near_ref[1])
    rhs_re = jnp.where(has_left(level), -made[:, :size], left_ref[0])
    rhs_im = jnp.where(has_left(level), -made[:, size:], left_ref[1])
    x = times(inv_re, inv_im, rhs_re, rhs_im)
    square = x * x
    both = square[:, :size] + square[:, size:]
    total = lax.dot_general(
        jnp.ones((8, size), F32),
        both,
        (((1,), (1,)), ((), ())),
        precision=HIGHEST,
        preferred_element_type=F32,
    )
    out_ref[...] = total * weight_ref[0]


def last_kernel(level, weight_ref, diag_ref, left_ref, right_ref, near_ref, out_ref):
    size = diag_ref.shape[-1]
    change = link_change(level, left_ref, right_ref, near_ref)
    inv_re, inv_im = inverse(diag_ref[0] - change[:, :size], diag_ref[1] - change[:, size:])
    finish(level, weight_ref, inv_re, inv_im, left_ref, near_ref, out_ref)


def last_invert_kernel(level, diag_ref, left_ref, right_ref, near_ref, inv_ref):
    size = diag_ref.shape[-1]
    change = link_change(level, left_ref, right_ref, near_ref)
    inv_ref[0], inv_ref[1] = inverse(
        diag_ref[0] - change[:, :size], diag_ref[1] - change[:, size:]
    )


def last_solve_kernel(level, weight_ref, inv_ref, left_ref, near_ref, out_ref):
    finish(level, weight_ref, inv_ref[0], inv_ref[1], left_ref, near_ref, out_ref)


def call(kernel, outs, specs, flops=0):
    return pl.pallas_call(
        kernel,
        out_shape=outs,
        in_specs=specs,
        out_specs=jax.tree.map(lambda _: pl.BlockSpec(memory_space=pltpu.VMEM), outs),
        compiler_params=pltpu.CompilerParams(vmem_limit_bytes=16 << 20),
        cost_estimate=pl.CostEstimate(flops=flops, bytes_accessed=1 << 20, transcendentals=0),
    )


def summed_over(value, axis):
    parts = lax.all_to_all(value, axis, 0, 0, tiled=True)
    return jnp.sum(parts, axis=0, keepdims=True)


def local(onsite, coupling, source_coupling, energy, broadening, weights):
    size = onsite.shape[2]
    devices = lax.axis_size("transpor")
    levels = devices.bit_length() - 1
    block = jax.ShapeDtypeStruct((2, size, size), F32)
    pair = jax.ShapeDtypeStruct((4, size, size), F32)
    behind = lax.ppermute(
        coupling, "transpor", [(s, (s + 1) % devices) for s in range(devices)]
    )
    position = lax.axis_index("transpor")
    contact = jnp.where(
        position == 0, source_coupling, jnp.where(position == devices - 1, coupling[0], 0.0)
    )

    def solved_at(level):
        return [block, block] if level in SPLIT_LEVELS else [pair]

    diag, inv = call(first_kernel, [block] * 2, [SMEM, SMEM] + vmem(2), 4 << 30)(
        energy, broadening, onsite, contact
    )
    left, right, *solved = call(start_kernel, [block, block] + solved_at(0), vmem(4))(
        inv, behind, coupling, source_coupling
    )
    for level in range(levels - 1):
        distance = 1 << level
        to_near = [(s, s ^ distance) for s in range(devices)]
        to_far = [
            (s, (s + (distance if s & distance else -distance)) % devices) for s in range(devices)
        ]
        near = lax.ppermute(solved[0], "transpor", to_near)
        far = lax.ppermute(solved[-1], "transpor", to_far)
        outs = [block, block] + solved_at(level + 1)
        if level in SPLIT_LEVELS:
            late_near = lax.ppermute(solved[1], "transpor", to_near)
            late_far = lax.ppermute(solved[0], "transpor", to_far)
            diag, inv = call(
                functools.partial(invert_kernel, level), [block, block], vmem(5), 4 << 30
            )(diag, left, right, near, far)
            left, right, *solved = call(functools.partial(couple_kernel, level), outs, vmem(5))(
                inv, left, right, late_near, late_far
            )
        else:
            diag, left, right, *solved = call(
                functools.partial(level_kernel, level), [block] + outs, vmem(5), 4 << 30
            )(diag, left, right, near, far)
    level = levels - 1
    to_near = [(s, s ^ (1 << level)) for s in range(devices)]
    near = lax.ppermute(solved[0], "transpor", to_near)
    count = lax.axis_size("energy")
    result = jax.ShapeDtypeStruct((8, size), F32)
    if level in SPLIT_LEVELS:
        late_near = lax.ppermute(solved[1], "transpor", to_near)
        inv = call(functools.partial(last_invert_kernel, level), block, vmem(4), 4 << 30)(
            diag, left, right, near
        )
        row = call(functools.partial(last_solve_kernel, level), result, [SMEM] + vmem(3))(
            weights, inv, left, late_near
        )
    else:
        row = call(functools.partial(last_kernel, level), result, [SMEM] + vmem(4))(
            weights, diag, left, right, near
        )
    return summed_over(row[0].reshape(count, size // count), "energy")


def solution(mesh):
    placed = (
        P("transpor", None, None, None),
        P("transpor", None, None, None),
        P(),
        P("energy"),
        P("energy"),
        P("energy"),
    )
    return jax.shard_map(
        local, mesh=mesh, in_specs=placed, out_specs=P("transpor", "energy"), check_vma=False
    )
```

```python
import functools

import jax
import jax.numpy as jnp
from jax import lax
from jax.experimental import pallas as pl
from jax.experimental.pallas import tpu as pltpu
from jax.sharding import PartitionSpec as P

F32 = jnp.float32
BF16 = jnp.bfloat16
HIGHEST = lax.Precision.HIGHEST
ROWS = 8
SPLIT_LEVELS = (0, 1, 2, 3, 4)


def dot(left, right):
    return jnp.dot(left, right, precision=HIGHEST, preferred_element_type=F32)


def row_of(value, k):
    return jnp.broadcast_to(value[k : k + 1, :], value.shape)


def column_of(value, j):
    index = jnp.full(value.shape, j, jnp.int32)
    return jnp.take_along_axis(value, index, axis=1, mode="promise_in_bounds")


def tree_sum(terms):
    terms = list(terms)
    while len(terms) > 1:
        paired = [terms[i] + terms[i + 1] for i in range(0, len(terms) - 1, 2)]
        terms = paired + terms[len(terms) - len(terms) % 2 :]
    return terms[0]


def mul(a, b):
    return a[0] * b[0] - a[1] * b[1], a[0] * b[1] + a[1] * b[0]


def mul_conj(a, b):
    return a[0] * b[0] + a[1] * b[1], a[1] * b[0] - a[0] * b[1]


def add(a, b):
    return a[0] + b[0], a[1] + b[1]


def sub(a, b):
    return a[0] - b[0], a[1] - b[1]


def chosen(where, a, b):
    return jnp.where(where, a[0], b[0]), jnp.where(where, a[1], b[1])


def eliminate_panel(columns, rows, place):
    columns, rows = list(columns), list(rows)
    zero = (0.0, 0.0)
    same = cross = None
    for k in range(0, ROWS, 2):
        x, y = columns[k], columns[k + 1]
        a, c = [tuple(row_of(part, k + r) for part in x) for r in range(2)]
        b, d = [tuple(row_of(part, k + r) for part in y) for r in range(2)]
        det = sub(mul(a, d), mul(b, c))
        inv = 1.0 / (det[0] * det[0] + det[1] * det[1])
        first, here = place == k, (place == k) | (place == k + 1)
        x, y = chosen(here, zero, x), chosen(here, zero, y)
        t0 = mul_conj(sub(mul(x, d), mul(y, c)), det)
        t1 = mul_conj(sub(mul(y, a), mul(x, b)), det)
        u0, u1 = (t0[0] * inv, t0[1] * inv), (t1[0] * inv, t1[1] * inv)
        for j in range(k + 2, ROWS):
            r0, r1 = [tuple(row_of(part, k + r) for part in columns[j]) for r in range(2)]
            if j < k + 4:
                w = add(mul(t0, r0), mul(t1, r1))
                columns[j] = sub(columns[j], (inv * w[0], inv * w[1]))
            else:
                columns[j] = sub(columns[j], add(mul(u0, r0), mul(u1, r1)))
        r0, r1 = [[row_of(part, k + r) for part in rows] for r in range(2)]
        taken = [
            (u0[0] * r0[q] + u0[1] * r0[q + 2]) + (u1[0] * r1[q] + u1[1] * r1[q + 2])
            for q in range(2)
        ] + [
            (u0[0] * r0[q + 2] - u0[1] * r0[q]) + (u1[0] * r1[q + 2] - u1[1] * r1[q])
            for q in range(2)
        ]
        rows = [part - change for part, change in zip(rows, taken)]
        scale = (det[0] * inv, -(det[1] * inv))
        p, q = mul(chosen(first, d, a), scale), mul(chosen(first, b, c), scale)
        same = p if k == 0 else chosen(here, p, same)
        cross = q if k == 0 else chosen(here, q, cross)
    odd = (place & 1) == 1
    other = [
        jnp.where(odd, pltpu.roll(part, 1, 0), pltpu.roll(part, ROWS - 1, 0)) for part in rows
    ]
    return [
        (same[0] * rows[q] + same[1] * rows[q + 2])
        - (cross[0] * other[q] + cross[1] * other[q + 2])
        for q in range(2)
    ] + [
        (same[0] * rows[q + 2] - same[1] * rows[q])
        - (cross[0] * other[q + 2] - cross[1] * other[q])
        for q in range(2)
    ]


def three_parts(value):
    high = value.astype(BF16)
    rest = value - high.astype(F32)
    middle = rest.astype(BF16)
    return high, middle, (rest - middle.astype(F32)).astype(BF16)


def short_dot(left, right):
    (l0, l1, l2), (r0, r1, r2) = left, right
    total = None
    for one, other, low, high in ((l2, l1, r0, r1), (l1, l0, r0, r2), (l0, l0, r1, r0)):
        part = jnp.dot(
            jnp.concatenate([one, other], 1),
            jnp.concatenate([low, high], 0),
            preferred_element_type=F32,
        )
        total = part if total is None else total + part
    return total


def inverse(re, im):
    size = re.shape[0]
    half = size // 2
    count = size // ROWS
    low = lax.broadcasted_iota(jnp.int32, (size, size), 1) < half
    halves = (
        jnp.where(low, re, pltpu.roll(im, half, 1)),
        jnp.where(low, pltpu.roll(re, half, 1), im),
    )
    a = [[part[ROWS * b : ROWS * (b + 1)] for part in halves] for b in range(count)]
    place = lax.broadcasted_iota(jnp.int32, (ROWS, size), 0)
    lane = lax.broadcasted_iota(jnp.int32, (ROWS, size), 1)
    empty = jnp.zeros((ROWS, 2 * size), F32)

    def gap(groups):
        return [jnp.zeros((2 * ROWS * groups, 2 * size), BF16)] if groups else []

    def times_i(part):
        turned = pltpu.roll(part, half, 1)
        return jnp.where(lane < half, -turned, turned)

    for t in range(count):
        side, base = divmod(ROWS * t, half)
        inside = (lane & (half - 1)) - base
        pivots = (inside >= 0) & (inside < ROWS)

        def cleared(block, q):
            return jnp.where(pivots, 0.0, a[block][q]) if q == side else a[block][q]

        def pivot_columns(block):
            part = a[block][side]
            return [
                (column_of(part, base + j), column_of(part, half + base + j)) for j in range(ROWS)
            ]

        rows = list(a[t]) + [times_i(part) for part in a[t]]
        rows[side] = jnp.where(pivots, (lane - base == place).astype(F32), rows[side])
        rows[side + 2] = jnp.where(
            pivots, (lane - half - base == place).astype(F32), rows[side + 2]
        )
        rows = eliminate_panel(pivot_columns(t), rows, place)
        ahead = t + 1
        if ahead < count:
            factors = pivot_columns(ahead)
            spread = [[row_of(part, j) for part in rows] for j in range(ROWS)]
            ahead_rows = [
                cleared(ahead, q)
                - tree_sum(
                    m[0] * row[q] + m[1] * row[q + 2] for m, row in zip(factors, spread)
                )
                for q in range(2)
            ]
        others = [b for b in range(count) if ahead == count or b not in (t, ahead)]
        left = three_parts(jnp.concatenate([a[b][side] for b in others], 0))
        group, second = divmod(base // ROWS, 2)
        groups = half // (2 * ROWS)
        right = []
        tops, lows = [
            three_parts(jnp.concatenate([empty, part] if second else [part, empty], 0))
            for part in (jnp.concatenate(rows[:2], 1), jnp.concatenate(rows[2:], 1))
        ]
        for top, bottom in zip(tops, lows):
            right.append(
                jnp.concatenate(
                    gap(group) + [top] + gap(groups - 1) + [bottom] + gap(groups - 1 - group), 0
                )
            )
        change = short_dot(left, right)
        for x, b in enumerate(others):
            part = change[ROWS * x : ROWS * (x + 1)]
            a[b] = [cleared(b, q) - part[:, q * size : (q + 1) * size] for q in range(2)]
        a[t] = rows[:2]
        if ahead < count:
            a[ahead] = ahead_rows
    return tuple(jnp.concatenate([block[q] for block in a], 0) for q in range(2))


def stacked(re, im):
    return jnp.concatenate(
        [jnp.concatenate([re, im], 1), jnp.concatenate([-im, re], 1)], 0
    )


def times(left_re, left_im, right_re, right_im):
    return dot(jnp.concatenate([left_re, left_im], 1), stacked(right_re, right_im))


def halves_times(halves, right_re, right_im):
    half = right_re.shape[0] // 2
    top = jnp.concatenate([right_re, right_im], 1)
    low = jnp.concatenate([-right_im, right_re], 1)
    return dot(
        jnp.concatenate(halves, 1),
        jnp.concatenate([top[:half], low[:half], top[half:], low[half:]], 0),
    )


def vmem(count):
    return [pl.BlockSpec(memory_space=pltpu.VMEM)] * count


SMEM = pl.BlockSpec(memory_space=pltpu.SMEM)


def first_kernel(energy_ref, broadening_ref, onsite_ref, contact_ref, diag_ref, inv_ref):
    size = onsite_ref.shape[-1]
    re, im, kr, ki = onsite_ref[0, 0], onsite_ref[0, 1], contact_ref[0], contact_ref[1]
    krt, kit = kr.T, ki.T
    gamma = times(kr, ki, krt, -kit)
    row = lax.broadcasted_iota(jnp.int32, (size, size), 0)
    col = lax.broadcasted_iota(jnp.int32, (size, size), 1)
    unit = (row == col).astype(F32)
    diag_re = energy_ref[0] * unit - 0.5 * (re + re.T) - 0.5 * gamma[:, size:]
    diag_im = broadening_ref[0] * unit - 0.5 * (im - im.T) + 0.5 * gamma[:, :size]
    diag_ref[0], diag_ref[1] = diag_re, diag_im
    inv_ref[0], inv_ref[1] = inverse(diag_re, diag_im)


def is_odd(level):
    return ((lax.axis_index("transpor") >> level) & 1) == 1


def solve_into(inv, left_re, left_im, right_re, right_im, solved_refs, level):
    size = left_re.shape[-1]
    left = halves_times(inv, left_re, left_im)
    right = halves_times(inv, right_re, right_im)
    if len(solved_refs) == 1:
        (solved_ref,) = solved_refs
        solved_ref[0], solved_ref[1] = left[:, :size], left[:, size:]
        solved_ref[2], solved_ref[3] = right[:, :size], right[:, size:]
    else:
        odd = is_odd(level)
        early, late = jnp.where(odd, left, right), jnp.where(odd, right, left)
        for ref, value in zip(solved_refs, (early, late)):
            ref[0], ref[1] = value[:, :size], value[:, size:]


def start_kernel(inv_ref, behind_ref, coupling_ref, source_ref, left_ref, right_ref, *solved_refs):
    place, count = lax.axis_index("transpor"), lax.axis_size("transpor")
    left_re = jnp.where(place == 0, source_ref[0], -behind_ref[0, 0].T)
    left_im = jnp.where(place == 0, source_ref[1], behind_ref[0, 1].T)
    right_re = jnp.where(place == count - 1, 0.0, -coupling_ref[0, 0])
    right_im = jnp.where(place == count - 1, 0.0, -coupling_ref[0, 1])
    left_ref[0], left_ref[1] = left_re, left_im
    right_ref[0], right_ref[1] = right_re, right_im
    solve_into((inv_ref[0], inv_ref[1]), left_re, left_im, right_re, right_im, solved_refs, 0)


def has_left(level):
    return lax.axis_index("transpor") >= (1 << level)


def either(odd, one, other):
    return [jnp.where(odd, one[k], other[k]) for k in range(2)]


def reduced_diag(level, diag_ref, left_ref, right_ref, across_left, across_right):
    size = diag_ref.shape[-1]
    across_left = [jnp.where(has_left(level), part, 0.0) for part in across_left]
    change = times(left_ref[0], left_ref[1], *across_left) + times(
        right_ref[0], right_ref[1], *across_right
    )
    return diag_ref[0] - change[:, :size], diag_ref[1] - change[:, size:]


def next_couplings(level, left_ref, right_ref, beyond_left, beyond_right):
    size = left_ref.shape[-1]
    made = times(left_ref[0], left_ref[1], *beyond_left)
    left_re = jnp.where(has_left(level), -made[:, :size], left_ref[0])
    left_im = jnp.where(has_left(level), -made[:, size:], left_ref[1])
    made = times(right_ref[0], right_ref[1], *beyond_right)
    return left_re, left_im, -made[:, :size], -made[:, size:]


def level_kernel(
    level,
    diag_ref,
    left_ref,
    right_ref,
    near_ref,
    far_ref,
    diag_out_ref,
    left_out_ref,
    right_out_ref,
    *solved_refs,
):
    odd = is_odd(level)
    near, far = near_ref, far_ref
    across_left = either(odd, near[2:], far[2:])
    across_right = either(odd, far[:2], near[:2])
    re, im = reduced_diag(level, diag_ref, left_ref, right_ref, across_left, across_right)
    diag_out_ref[0], diag_out_ref[1] = re, im
    beyond_left = either(odd, near[:2], far[:2])
    beyond_right = either(odd, far[2:], near[2:])
    blocks = next_couplings(level, left_ref, right_ref, beyond_left, beyond_right)
    left_out_ref[0], left_out_ref[1], right_out_ref[0], right_out_ref[1] = blocks
    solve_into(inverse(re, im), *blocks, solved_refs, level + 1)


def invert_kernel(
    level, diag_ref, left_ref, right_ref, near_ref, far_ref, diag_out_ref, inv_ref
):
    odd = is_odd(level)
    across_left = either(odd, near_ref, far_ref)
    across_right = either(odd, far_ref, near_ref)
    re, im = reduced_diag(level, diag_ref, left_ref, right_ref, across_left, across_right)
    diag_out_ref[0], diag_out_ref[1] = re, im
    inv_ref[0], inv_ref[1] = inverse(re, im)


def couple_kernel(
    level,
    inv_ref,
    left_ref,
    right_ref,
    near_ref,
    far_ref,
    left_out_ref,
    right_out_ref,
    *solved_refs,
):
    odd = is_odd(level)
    beyond_left = either(odd, near_ref, far_ref)
    beyond_right = either(odd, far_ref, near_ref)
    blocks = next_couplings(level, left_ref, right_ref, beyond_left, beyond_right)
    left_out_ref[0], left_out_ref[1], right_out_ref[0], right_out_ref[1] = blocks
    solve_into((inv_ref[0], inv_ref[1]), *blocks, solved_refs, level + 1)


def link_change(level, left_ref, right_ref, near_ref):
    reached = has_left(level)
    link = [jnp.where(reached, left_ref[k], right_ref[k]) for k in range(2)]
    if near_ref.shape[0] == 2:
        return times(*link, near_ref[0], near_ref[1])
    return times(*link, *(jnp.where(reached, near_ref[k + 2], near_ref[k]) for k in range(2)))


def finish(level, weight_ref, inv, left_ref, near_ref, out_ref):
    size = left_ref.shape[-1]
    made = times(left_ref[0], left_ref[1], near_ref[0], near_ref[1])
    rhs_re = jnp.where(has_left(level), -made[:, :size], left_ref[0])
    rhs_im = jnp.where(has_left(level), -made[:, size:], left_ref[1])
    x = halves_times(inv, rhs_re, rhs_im)
    square = x * x
    both = square[:, :size] + square[:, size:]
    total = lax.dot_general(
        jnp.ones((8, size), F32),
        both,
        (((1,), (1,)), ((), ())),
        precision=HIGHEST,
        preferred_element_type=F32,
    )
    out_ref[...] = total * weight_ref[0]


def last_kernel(level, weight_ref, diag_ref, left_ref, right_ref, near_ref, out_ref):
    size = diag_ref.shape[-1]
    change = link_change(level, left_ref, right_ref, near_ref)
    inv = inverse(diag_ref[0] - change[:, :size], diag_ref[1] - change[:, size:])
    finish(level, weight_ref, inv, left_ref, near_ref, out_ref)


def last_invert_kernel(level, diag_ref, left_ref, right_ref, near_ref, inv_ref):
    size = diag_ref.shape[-1]
    change = link_change(level, left_ref, right_ref, near_ref)
    inv_ref[0], inv_ref[1] = inverse(
        diag_ref[0] - change[:, :size], diag_ref[1] - change[:, size:]
    )


def last_solve_kernel(level, weight_ref, inv_ref, left_ref, near_ref, out_ref):
    finish(level, weight_ref, (inv_ref[0], inv_ref[1]), left_ref, near_ref, out_ref)


def call(kernel, outs, specs, flops=0):
    return pl.pallas_call(
        kernel,
        out_shape=outs,
        in_specs=specs,
        out_specs=jax.tree.map(lambda _: pl.BlockSpec(memory_space=pltpu.VMEM), outs),
        compiler_params=pltpu.CompilerParams(vmem_limit_bytes=16 << 20),
        cost_estimate=pl.CostEstimate(flops=flops, bytes_accessed=1 << 20, transcendentals=0),
    )


def summed_over(value, axis):
    parts = lax.all_to_all(value, axis, 0, 0, tiled=True)
    return jnp.sum(parts, axis=0, keepdims=True)


def local(onsite, coupling, source_coupling, energy, broadening, weights):
    size = onsite.shape[2]
    devices = lax.axis_size("transpor")
    levels = devices.bit_length() - 1
    block = jax.ShapeDtypeStruct((2, size, size), F32)
    pair = jax.ShapeDtypeStruct((4, size, size), F32)
    behind = lax.ppermute(
        coupling, "transpor", [(s, (s + 1) % devices) for s in range(devices)]
    )
    position = lax.axis_index("transpor")
    contact = jnp.where(
        position == 0, source_coupling, jnp.where(position == devices - 1, coupling[0], 0.0)
    )

    def solved_at(level):
        return [block, block] if level in SPLIT_LEVELS else [pair]

    diag, inv = call(first_kernel, [block] * 2, [SMEM, SMEM] + vmem(2), 4 << 30)(
        energy, broadening, onsite, contact
    )
    left, right, *solved = call(start_kernel, [block, block] + solved_at(0), vmem(4))(
        inv, behind, coupling, source_coupling
    )
    for level in range(levels - 1):
        distance = 1 << level
        to_near = [(s, s ^ distance) for s in range(devices)]
        to_far = [
            (s, (s + (distance if s & distance else -distance)) % devices) for s in range(devices)
        ]
        near = lax.ppermute(solved[0], "transpor", to_near)
        far = lax.ppermute(solved[-1], "transpor", to_far)
        outs = [block, block] + solved_at(level + 1)
        if level in SPLIT_LEVELS:
            late_near = lax.ppermute(solved[1], "transpor", to_near)
            late_far = lax.ppermute(solved[0], "transpor", to_far)
            diag, inv = call(
                functools.partial(invert_kernel, level), [block, block], vmem(5), 4 << 30
            )(diag, left, right, near, far)
            left, right, *solved = call(functools.partial(couple_kernel, level), outs, vmem(5))(
                inv, left, right, late_near, late_far
            )
        else:
            diag, left, right, *solved = call(
                functools.partial(level_kernel, level), [block] + outs, vmem(5), 4 << 30
            )(diag, left, right, near, far)
    level = levels - 1
    to_near = [(s, s ^ (1 << level)) for s in range(devices)]
    near = lax.ppermute(solved[0], "transpor", to_near)
    count = lax.axis_size("energy")
    result = jax.ShapeDtypeStruct((8, size), F32)
    if level in SPLIT_LEVELS:
        late_near = lax.ppermute(solved[1], "transpor", to_near)
        inv = call(functools.partial(last_invert_kernel, level), block, vmem(4), 4 << 30)(
            diag, left, right, near
        )
        row = call(functools.partial(last_solve_kernel, level), result, [SMEM] + vmem(3))(
            weights, inv, left, late_near
        )
    else:
        row = call(functools.partial(last_kernel, level), result, [SMEM] + vmem(4))(
            weights, diag, left, right, near
        )
    return summed_over(row[0].reshape(count, size // count), "energy")


def solution(mesh):
    placed = (
        P("transpor", None, None, None),
        P("transpor", None, None, None),
        P(),
        P("energy"),
        P("energy"),
        P("energy"),
    )
    return jax.shard_map(
        local, mesh=mesh, in_specs=placed, out_specs=P("transpor", "energy"), check_vma=False
    )
```

```python
import functools

import jax
import jax.numpy as jnp
from jax import lax
from jax.experimental import pallas as pl
from jax.experimental.pallas import tpu as pltpu
from jax.sharding import PartitionSpec as P

F32 = jnp.float32
BF16 = jnp.bfloat16
HIGHEST = lax.Precision.HIGHEST
ROWS = 8
SPLIT_LEVELS = (0, 1, 2, 3, 4)


def dot(left, right):
    return jnp.dot(left, right, precision=HIGHEST, preferred_element_type=F32)


def row_of(value, k):
    return jnp.broadcast_to(value[k : k + 1, :], value.shape)


def column_of(value, j):
    index = jnp.full(value.shape, j, jnp.int32)
    return jnp.take_along_axis(value, index, axis=1, mode="promise_in_bounds")


def tree_sum(terms):
    terms = list(terms)
    while len(terms) > 1:
        paired = [terms[i] + terms[i + 1] for i in range(0, len(terms) - 1, 2)]
        terms = paired + terms[len(terms) - len(terms) % 2 :]
    return terms[0]


def mul(a, b):
    return a[0] * b[0] - a[1] * b[1], a[0] * b[1] + a[1] * b[0]


def mul_conj(a, b):
    return a[0] * b[0] + a[1] * b[1], a[1] * b[0] - a[0] * b[1]


def add(a, b):
    return a[0] + b[0], a[1] + b[1]


def sub(a, b):
    return a[0] - b[0], a[1] - b[1]


def chosen(where, a, b):
    return jnp.where(where, a[0], b[0]), jnp.where(where, a[1], b[1])


def eliminate_panel(columns, rows, place):
    columns, rows = list(columns), list(rows)
    zero = (0.0, 0.0)
    same = cross = None
    for k in range(0, ROWS, 2):
        x, y = columns[k], columns[k + 1]
        a, c = [tuple(row_of(part, k + r) for part in x) for r in range(2)]
        b, d = [tuple(row_of(part, k + r) for part in y) for r in range(2)]
        det = sub(mul(a, d), mul(b, c))
        inv = 1.0 / (det[0] * det[0] + det[1] * det[1])
        first, here = place == k, (place == k) | (place == k + 1)
        x, y = chosen(here, zero, x), chosen(here, zero, y)
        t0 = mul_conj(sub(mul(x, d), mul(y, c)), det)
        t1 = mul_conj(sub(mul(y, a), mul(x, b)), det)
        u0, u1 = (t0[0] * inv, t0[1] * inv), (t1[0] * inv, t1[1] * inv)
        for j in range(k + 2, ROWS):
            r0, r1 = [tuple(row_of(part, k + r) for part in columns[j]) for r in range(2)]
            if j < k + 4:
                w = add(mul(t0, r0), mul(t1, r1))
                columns[j] = sub(columns[j], (inv * w[0], inv * w[1]))
            else:
                columns[j] = sub(columns[j], add(mul(u0, r0), mul(u1, r1)))
        r0, r1 = [[row_of(part, k + r) for part in rows] for r in range(2)]
        taken = [
            (u0[0] * r0[q] + u0[1] * r0[q + 2]) + (u1[0] * r1[q] + u1[1] * r1[q + 2])
            for q in range(2)
        ] + [
            (u0[0] * r0[q + 2] - u0[1] * r0[q]) + (u1[0] * r1[q + 2] - u1[1] * r1[q])
            for q in range(2)
        ]
        rows = [part - change for part, change in zip(rows, taken)]
        scale = (det[0] * inv, -(det[1] * inv))
        p, q = mul(chosen(first, d, a), scale), mul(chosen(first, b, c), scale)
        same = p if k == 0 else chosen(here, p, same)
        cross = q if k == 0 else chosen(here, q, cross)
    odd = (place & 1) == 1
    other = [
        jnp.where(odd, pltpu.roll(part, 1, 0), pltpu.roll(part, ROWS - 1, 0)) for part in rows
    ]
    return [
        (same[0] * rows[q] + same[1] * rows[q + 2])
        - (cross[0] * other[q] + cross[1] * other[q + 2])
        for q in range(2)
    ] + [
        (same[0] * rows[q + 2] - same[1] * rows[q])
        - (cross[0] * other[q + 2] - cross[1] * other[q])
        for q in range(2)
    ]


def three_parts(value):
    high = value.astype(BF16)
    rest = value - high.astype(F32)
    middle = rest.astype(BF16)
    return high, middle, (rest - middle.astype(F32)).astype(BF16)


def short_dot(left, right):
    (l0, l1, l2), (r0, r1, r2) = left, right
    total = None
    for one, other, low, high in ((l2, l1, r0, r1), (l1, l0, r0, r2), (l0, l0, r1, r0)):
        part = jnp.dot(
            jnp.concatenate([one, other], 1),
            jnp.concatenate([low, high], 0),
            preferred_element_type=F32,
        )
        total = part if total is None else total + part
    return total


def inverse(re, im):
    size = re.shape[0]
    half = size // 2
    count = size // ROWS
    low = lax.broadcasted_iota(jnp.int32, (size, size), 1) < half
    halves = (
        jnp.where(low, re, pltpu.roll(im, half, 1)),
        jnp.where(low, pltpu.roll(re, half, 1), im),
    )
    a = [[part[ROWS * b : ROWS * (b + 1)] for part in halves] for b in range(count)]
    place = lax.broadcasted_iota(jnp.int32, (ROWS, size), 0)
    lane = lax.broadcasted_iota(jnp.int32, (ROWS, size), 1)
    empty = jnp.zeros((ROWS, 2 * size), F32)

    def gap(groups):
        return [jnp.zeros((2 * ROWS * groups, 2 * size), BF16)] if groups else []

    def times_i(part):
        turned = pltpu.roll(part, half, 1)
        return jnp.where(lane < half, -turned, turned)

    for t in range(count):
        side, base = divmod(ROWS * t, half)
        inside = (lane & (half - 1)) - base
        pivots = (inside >= 0) & (inside < ROWS)

        def cleared(block, q):
            return jnp.where(pivots, 0.0, a[block][q]) if q == side else a[block][q]

        def pivot_columns(block):
            part = a[block][side]
            return [
                (column_of(part, base + j), column_of(part, half + base + j)) for j in range(ROWS)
            ]

        rows = list(a[t]) + [times_i(part) for part in a[t]]
        rows[side] = jnp.where(pivots, (lane - base == place).astype(F32), rows[side])
        rows[side + 2] = jnp.where(
            pivots, (lane - half - base == place).astype(F32), rows[side + 2]
        )
        rows = eliminate_panel(pivot_columns(t), rows, place)
        ahead = t + 1
        if ahead < count:
            factors = pivot_columns(ahead)
            spread = [[row_of(part, j) for part in rows] for j in range(ROWS)]
            ahead_rows = [
                cleared(ahead, q)
                - tree_sum(
                    m[0] * row[q] + m[1] * row[q + 2] for m, row in zip(factors, spread)
                )
                for q in range(2)
            ]
        others = [b for b in range(count) if ahead == count or b not in (t, ahead)]
        left = three_parts(jnp.concatenate([a[b][side] for b in others], 0))
        group, second = divmod(base // ROWS, 2)
        groups = half // (2 * ROWS)
        right = []
        tops, lows = [
            three_parts(jnp.concatenate([empty, part] if second else [part, empty], 0))
            for part in (jnp.concatenate(rows[:2], 1), jnp.concatenate(rows[2:], 1))
        ]
        for top, bottom in zip(tops, lows):
            right.append(
                jnp.concatenate(
                    gap(group) + [top] + gap(groups - 1) + [bottom] + gap(groups - 1 - group), 0
                )
            )
        change = short_dot(left, right)
        for x, b in enumerate(others):
            part = change[ROWS * x : ROWS * (x + 1)]
            a[b] = [cleared(b, q) - part[:, q * size : (q + 1) * size] for q in range(2)]
        a[t] = rows[:2]
        if ahead < count:
            a[ahead] = ahead_rows
    return tuple(jnp.concatenate([block[q] for block in a], 0) for q in range(2))


def stacked(re, im):
    return jnp.concatenate(
        [jnp.concatenate([re, im], 1), jnp.concatenate([-im, re], 1)], 0
    )


def times(left_re, left_im, right_re, right_im):
    return dot(jnp.concatenate([left_re, left_im], 1), stacked(right_re, right_im))


def halves_times(halves, right_re, right_im):
    half = right_re.shape[0] // 2
    top = jnp.concatenate([right_re, right_im], 1)
    low = jnp.concatenate([-right_im, right_re], 1)
    return dot(
        jnp.concatenate(halves, 1),
        jnp.concatenate([top[:half], low[:half], top[half:], low[half:]], 0),
    )


def vmem(count):
    return [pl.BlockSpec(memory_space=pltpu.VMEM)] * count


SMEM = pl.BlockSpec(memory_space=pltpu.SMEM)


def first_kernel(energy_ref, broadening_ref, onsite_ref, contact_ref, diag_ref, inv_ref):
    size = onsite_ref.shape[-1]
    re, im, kr, ki = onsite_ref[0, 0], onsite_ref[0, 1], contact_ref[0], contact_ref[1]
    krt, kit = kr.T, ki.T
    gamma = times(kr, ki, krt, -kit)
    row = lax.broadcasted_iota(jnp.int32, (size, size), 0)
    col = lax.broadcasted_iota(jnp.int32, (size, size), 1)
    unit = (row == col).astype(F32)
    diag_re = energy_ref[0] * unit - 0.5 * (re + re.T) - 0.5 * gamma[:, size:]
    diag_im = broadening_ref[0] * unit - 0.5 * (im - im.T) + 0.5 * gamma[:, :size]
    diag_ref[0], diag_ref[1] = diag_re, diag_im
    inv_ref[0], inv_ref[1] = inverse(diag_re, diag_im)


def is_odd(level):
    return ((lax.axis_index("transpor") >> level) & 1) == 1


def solve_into(inv, left_re, left_im, right_re, right_im, solved_refs, level):
    size = left_re.shape[-1]
    left = halves_times(inv, left_re, left_im)
    right = halves_times(inv, right_re, right_im)
    if len(solved_refs) == 1:
        (solved_ref,) = solved_refs
        solved_ref[0], solved_ref[1] = left[:, :size], left[:, size:]
        solved_ref[2], solved_ref[3] = right[:, :size], right[:, size:]
    else:
        odd = is_odd(level)
        early, late = jnp.where(odd, left, right), jnp.where(odd, right, left)
        for ref, value in zip(solved_refs, (early, late)):
            ref[0], ref[1] = value[:, :size], value[:, size:]


def start_kernel(inv_ref, behind_ref, coupling_ref, source_ref, left_ref, right_ref, *solved_refs):
    place, count = lax.axis_index("transpor"), lax.axis_size("transpor")
    left_re = jnp.where(place == 0, source_ref[0], -behind_ref[0, 0].T)
    left_im = jnp.where(place == 0, source_ref[1], behind_ref[0, 1].T)
    right_re = jnp.where(place == count - 1, 0.0, -coupling_ref[0, 0])
    right_im = jnp.where(place == count - 1, 0.0, -coupling_ref[0, 1])
    left_ref[0], left_ref[1] = left_re, left_im
    right_ref[0], right_ref[1] = right_re, right_im
    solve_into((inv_ref[0], inv_ref[1]), left_re, left_im, right_re, right_im, solved_refs, 0)


def has_left(level):
    return lax.axis_index("transpor") >= (1 << level)


def either(odd, one, other):
    return [jnp.where(odd, one[k], other[k]) for k in range(2)]


def reduced_diag(level, diag_ref, left_ref, right_ref, across_left, across_right):
    size = diag_ref.shape[-1]
    across_left = [jnp.where(has_left(level), part, 0.0) for part in across_left]
    change = times(left_ref[0], left_ref[1], *across_left) + times(
        right_ref[0], right_ref[1], *across_right
    )
    return diag_ref[0] - change[:, :size], diag_ref[1] - change[:, size:]


def next_couplings(level, left_ref, right_ref, beyond_left, beyond_right):
    size = left_ref.shape[-1]
    made = times(left_ref[0], left_ref[1], *beyond_left)
    left_re = jnp.where(has_left(level), -made[:, :size], left_ref[0])
    left_im = jnp.where(has_left(level), -made[:, size:], left_ref[1])
    made = times(right_ref[0], right_ref[1], *beyond_right)
    return left_re, left_im, -made[:, :size], -made[:, size:]


def level_kernel(
    level,
    diag_ref,
    left_ref,
    right_ref,
    near_ref,
    far_ref,
    diag_out_ref,
    left_out_ref,
    right_out_ref,
    *solved_refs,
):
    odd = is_odd(level)
    near, far = near_ref, far_ref
    across_left = either(odd, near[2:], far[2:])
    across_right = either(odd, far[:2], near[:2])
    re, im = reduced_diag(level, diag_ref, left_ref, right_ref, across_left, across_right)
    diag_out_ref[0], diag_out_ref[1] = re, im
    beyond_left = either(odd, near[:2], far[:2])
    beyond_right = either(odd, far[2:], near[2:])
    blocks = next_couplings(level, left_ref, right_ref, beyond_left, beyond_right)
    left_out_ref[0], left_out_ref[1], right_out_ref[0], right_out_ref[1] = blocks
    solve_into(inverse(re, im), *blocks, solved_refs, level + 1)


def invert_kernel(
    level, diag_ref, left_ref, right_ref, near_ref, far_ref, diag_out_ref, inv_ref
):
    odd = is_odd(level)
    across_left = either(odd, near_ref, far_ref)
    across_right = either(odd, far_ref, near_ref)
    re, im = reduced_diag(level, diag_ref, left_ref, right_ref, across_left, across_right)
    diag_out_ref[0], diag_out_ref[1] = re, im
    inv_ref[0], inv_ref[1] = inverse(re, im)


def couple_kernel(
    level,
    inv_ref,
    left_ref,
    right_ref,
    near_ref,
    far_ref,
    left_out_ref,
    right_out_ref,
    *solved_refs,
):
    odd = is_odd(level)
    beyond_left = either(odd, near_ref, far_ref)
    beyond_right = either(odd, far_ref, near_ref)
    blocks = next_couplings(level, left_ref, right_ref, beyond_left, beyond_right)
    left_out_ref[0], left_out_ref[1], right_out_ref[0], right_out_ref[1] = blocks
    solve_into((inv_ref[0], inv_ref[1]), *blocks, solved_refs, level + 1)


def link_change(level, left_ref, right_ref, near_ref):
    reached = has_left(level)
    link = [jnp.where(reached, left_ref[k], right_ref[k]) for k in range(2)]
    if near_ref.shape[0] == 2:
        return times(*link, near_ref[0], near_ref[1])
    return times(*link, *(jnp.where(reached, near_ref[k + 2], near_ref[k]) for k in range(2)))


def finish(level, inv, left_ref, near_ref, out_ref):
    size = left_ref.shape[-1]
    made = times(left_ref[0], left_ref[1], near_ref[0], near_ref[1])
    rhs_re = jnp.where(has_left(level), -made[:, :size], left_ref[0])
    rhs_im = jnp.where(has_left(level), -made[:, size:], left_ref[1])
    x = halves_times(inv, rhs_re, rhs_im)
    square = x * x
    both = square[:, :size] + square[:, size:]
    total = lax.dot_general(
        jnp.ones((8, size), F32),
        both,
        (((1,), (1,)), ((), ())),
        precision=HIGHEST,
        preferred_element_type=F32,
    )
    out_ref[...] = total


def last_kernel(level, diag_ref, left_ref, right_ref, near_ref, out_ref):
    size = diag_ref.shape[-1]
    change = link_change(level, left_ref, right_ref, near_ref)
    inv = inverse(diag_ref[0] - change[:, :size], diag_ref[1] - change[:, size:])
    finish(level, inv, left_ref, near_ref, out_ref)


def last_invert_kernel(level, diag_ref, left_ref, right_ref, near_ref, inv_ref):
    size = diag_ref.shape[-1]
    change = link_change(level, left_ref, right_ref, near_ref)
    inv_ref[0], inv_ref[1] = inverse(
        diag_ref[0] - change[:, :size], diag_ref[1] - change[:, size:]
    )


def last_solve_kernel(level, inv_ref, left_ref, near_ref, out_ref):
    finish(level, (inv_ref[0], inv_ref[1]), left_ref, near_ref, out_ref)


def call(kernel, outs, specs, flops=0):
    return pl.pallas_call(
        kernel,
        out_shape=outs,
        in_specs=specs,
        out_specs=jax.tree.map(lambda _: pl.BlockSpec(memory_space=pltpu.VMEM), outs),
        compiler_params=pltpu.CompilerParams(vmem_limit_bytes=16 << 20),
        cost_estimate=pl.CostEstimate(flops=flops, bytes_accessed=1 << 20, transcendentals=0),
    )


def summed_over(value, axis):
    parts = lax.all_to_all(value, axis, 0, 0, tiled=True)
    return jnp.sum(parts, axis=0, keepdims=True)


def local(onsite, coupling, source_coupling, energy, broadening, weights):
    size = onsite.shape[2]
    devices = lax.axis_size("transpor")
    levels = devices.bit_length() - 1
    block = jax.ShapeDtypeStruct((2, size, size), F32)
    pair = jax.ShapeDtypeStruct((4, size, size), F32)
    behind = lax.ppermute(
        coupling, "transpor", [(s, (s + 1) % devices) for s in range(devices)]
    )
    position = lax.axis_index("transpor")
    contact = jnp.where(
        position == 0, source_coupling, jnp.where(position == devices - 1, coupling[0], 0.0)
    )

    def solved_at(level):
        return [block, block] if level in SPLIT_LEVELS else [pair]

    diag, inv = call(first_kernel, [block] * 2, [SMEM, SMEM] + vmem(2), 4 << 30)(
        energy, broadening, onsite, contact
    )
    left, right, *solved = call(start_kernel, [block, block] + solved_at(0), vmem(4))(
        inv, behind, coupling, source_coupling
    )
    for level in range(levels - 1):
        distance = 1 << level
        to_near = [(s, s ^ distance) for s in range(devices)]
        to_far = [
            (s, (s + (distance if s & distance else -distance)) % devices) for s in range(devices)
        ]
        near = lax.ppermute(solved[0], "transpor", to_near)
        far = lax.ppermute(solved[-1], "transpor", to_far)
        outs = [block, block] + solved_at(level + 1)
        if level in SPLIT_LEVELS:
            late = solved
            if level == 2:
                near, *late = lax.optimization_barrier((near, *solved))
            late_near = lax.ppermute(late[1], "transpor", to_near)
            late_far = lax.ppermute(late[0], "transpor", to_far)
            diag, inv = call(
                functools.partial(invert_kernel, level), [block, block], vmem(5), 4 << 30
            )(diag, left, right, near, far)
            left, right, *solved = call(functools.partial(couple_kernel, level), outs, vmem(5))(
                inv, left, right, late_near, late_far
            )
        else:
            diag, left, right, *solved = call(
                functools.partial(level_kernel, level), [block] + outs, vmem(5), 4 << 30
            )(diag, left, right, near, far)
    level = levels - 1
    to_near = [(s, s ^ (1 << level)) for s in range(devices)]
    near = lax.ppermute(solved[0], "transpor", to_near)
    count = lax.axis_size("energy")
    result = jax.ShapeDtypeStruct((8, size), F32)
    if level in SPLIT_LEVELS:
        late_near = lax.ppermute(solved[1], "transpor", to_near)
        inv = call(functools.partial(last_invert_kernel, level), block, vmem(4), 4 << 30)(
            diag, left, right, near
        )
        row = call(functools.partial(last_solve_kernel, level), result, vmem(3))(
            inv, left, late_near
        )
    else:
        row = call(functools.partial(last_kernel, level), result, vmem(4))(
            diag, left, right, near
        )
    weighted = weights[0] * row[0]
    return summed_over(weighted.reshape(count, size // count), "energy")


def solution(mesh):
    placed = (
        P("transpor", None, None, None),
        P("transpor", None, None, None),
        P(),
        P("energy"),
        P("energy"),
        P("energy"),
    )
    return jax.shard_map(
        local, mesh=mesh, in_specs=placed, out_specs=P("transpor", "energy"), check_vma=False
    )
```

```python
import functools

import jax
import jax.numpy as jnp
from jax import lax
from jax.experimental import pallas as pl
from jax.experimental.pallas import tpu as pltpu
from jax.sharding import PartitionSpec as P

F32 = jnp.float32
BF16 = jnp.bfloat16
HIGHEST = lax.Precision.HIGHEST
ROWS = 8
SPLIT_LEVELS = (0, 1, 2, 3, 4)


def dot(left, right):
    return jnp.dot(left, right, precision=HIGHEST, preferred_element_type=F32)


def row_of(value, k):
    return jnp.broadcast_to(value[k : k + 1, :], value.shape)


def column_of(value, j):
    index = jnp.full(value.shape, j, jnp.int32)
    return jnp.take_along_axis(value, index, axis=1, mode="promise_in_bounds")


def tree_sum(terms):
    terms = list(terms)
    while len(terms) > 1:
        paired = [terms[i] + terms[i + 1] for i in range(0, len(terms) - 1, 2)]
        terms = paired + terms[len(terms) - len(terms) % 2 :]
    return terms[0]


def mul(a, b):
    return a[0] * b[0] - a[1] * b[1], a[0] * b[1] + a[1] * b[0]


def mul_conj(a, b):
    return a[0] * b[0] + a[1] * b[1], a[1] * b[0] - a[0] * b[1]


def add(a, b):
    return a[0] + b[0], a[1] + b[1]


def sub(a, b):
    return a[0] - b[0], a[1] - b[1]


def chosen(where, a, b):
    return jnp.where(where, a[0], b[0]), jnp.where(where, a[1], b[1])


def eliminate_panel(columns, rows, place):
    columns, rows = list(columns), list(rows)
    zero = (0.0, 0.0)
    same = cross = None
    for k in range(0, ROWS, 2):
        x, y = columns[k], columns[k + 1]
        a, c = [tuple(row_of(part, k + r) for part in x) for r in range(2)]
        b, d = [tuple(row_of(part, k + r) for part in y) for r in range(2)]
        det = sub(mul(a, d), mul(b, c))
        inv = 1.0 / (det[0] * det[0] + det[1] * det[1])
        first, here = place == k, (place == k) | (place == k + 1)
        x, y = chosen(here, zero, x), chosen(here, zero, y)
        t0 = mul_conj(sub(mul(x, d), mul(y, c)), det)
        t1 = mul_conj(sub(mul(y, a), mul(x, b)), det)
        u0, u1 = (t0[0] * inv, t0[1] * inv), (t1[0] * inv, t1[1] * inv)
        for j in range(k + 2, ROWS):
            r0, r1 = [tuple(row_of(part, k + r) for part in columns[j]) for r in range(2)]
            if j < k + 4:
                w = add(mul(t0, r0), mul(t1, r1))
                columns[j] = sub(columns[j], (inv * w[0], inv * w[1]))
            else:
                columns[j] = sub(columns[j], add(mul(u0, r0), mul(u1, r1)))
        r0, r1 = [[row_of(part, k + r) for part in rows] for r in range(2)]
        taken = [
            (u0[0] * r0[q] + u0[1] * r0[q + 2]) + (u1[0] * r1[q] + u1[1] * r1[q + 2])
            for q in range(2)
        ] + [
            (u0[0] * r0[q + 2] - u0[1] * r0[q]) + (u1[0] * r1[q + 2] - u1[1] * r1[q])
            for q in range(2)
        ]
        rows = [part - change for part, change in zip(rows, taken)]
        scale = (det[0] * inv, -(det[1] * inv))
        p, q = mul(chosen(first, d, a), scale), mul(chosen(first, b, c), scale)
        same = p if k == 0 else chosen(here, p, same)
        cross = q if k == 0 else chosen(here, q, cross)
    odd = (place & 1) == 1
    other = [
        jnp.where(odd, pltpu.roll(part, 1, 0), pltpu.roll(part, ROWS - 1, 0)) for part in rows
    ]
    return [
        (same[0] * rows[q] + same[1] * rows[q + 2])
        - (cross[0] * other[q] + cross[1] * other[q + 2])
        for q in range(2)
    ] + [
        (same[0] * rows[q + 2] - same[1] * rows[q])
        - (cross[0] * other[q + 2] - cross[1] * other[q])
        for q in range(2)
    ]


def three_parts(value):
    high = value.astype(BF16)
    rest = value - high.astype(F32)
    middle = rest.astype(BF16)
    return high, middle, (rest - middle.astype(F32)).astype(BF16)


def short_dot(left, right):
    (l0, l1, l2), (r0, r1, r2) = left, right
    total = None
    for one, other, low, high in ((l2, l1, r0, r1), (l1, l0, r0, r2), (l0, l0, r1, r0)):
        part = jnp.dot(
            jnp.concatenate([one, other], 1),
            jnp.concatenate([low, high], 0),
            preferred_element_type=F32,
        )
        total = part if total is None else total + part
    return total


def inverse(re, im):
    size = re.shape[0]
    half = size // 2
    count = size // ROWS
    low = lax.broadcasted_iota(jnp.int32, (size, size), 1) < half
    halves = (
        jnp.where(low, re, pltpu.roll(im, half, 1)),
        jnp.where(low, pltpu.roll(re, half, 1), im),
    )
    a = [[part[ROWS * b : ROWS * (b + 1)] for part in halves] for b in range(count)]
    place = lax.broadcasted_iota(jnp.int32, (ROWS, size), 0)
    lane = lax.broadcasted_iota(jnp.int32, (ROWS, size), 1)
    empty = jnp.zeros((ROWS, 2 * size), F32)

    def gap(groups):
        return [jnp.zeros((2 * ROWS * groups, 2 * size), BF16)] if groups else []

    def times_i(part):
        turned = pltpu.roll(part, half, 1)
        return jnp.where(lane < half, -turned, turned)

    for t in range(count):
        side, base = divmod(ROWS * t, half)
        inside = (lane & (half - 1)) - base
        pivots = (inside >= 0) & (inside < ROWS)

        def cleared(block, q):
            return jnp.where(pivots, 0.0, a[block][q]) if q == side else a[block][q]

        def pivot_columns(block):
            part = a[block][side]
            return [
                (column_of(part, base + j), column_of(part, half + base + j)) for j in range(ROWS)
            ]

        rows = list(a[t]) + [times_i(part) for part in a[t]]
        rows[side] = jnp.where(pivots, (lane - base == place).astype(F32), rows[side])
        rows[side + 2] = jnp.where(
            pivots, (lane - half - base == place).astype(F32), rows[side + 2]
        )
        rows = eliminate_panel(pivot_columns(t), rows, place)
        ahead = t + 1
        if ahead < count:
            factors = pivot_columns(ahead)
            spread = [[row_of(part, j) for part in rows] for j in range(ROWS)]
            ahead_rows = [
                cleared(ahead, q)
                - tree_sum(
                    m[0] * row[q] + m[1] * row[q + 2] for m, row in zip(factors, spread)
                )
                for q in range(2)
            ]
        others = [b for b in range(count) if ahead == count or b not in (t, ahead)]
        left = three_parts(jnp.concatenate([a[b][side] for b in others], 0))
        group, second = divmod(base // ROWS, 2)
        groups = half // (2 * ROWS)
        right = []
        tops, lows = [
            three_parts(jnp.concatenate([empty, part] if second else [part, empty], 0))
            for part in (jnp.concatenate(rows[:2], 1), jnp.concatenate(rows[2:], 1))
        ]
        for top, bottom in zip(tops, lows):
            right.append(
                jnp.concatenate(
                    gap(group) + [top] + gap(groups - 1) + [bottom] + gap(groups - 1 - group), 0
                )
            )
        change = short_dot(left, right)
        for x, b in enumerate(others):
            part = change[ROWS * x : ROWS * (x + 1)]
            a[b] = [cleared(b, q) - part[:, q * size : (q + 1) * size] for q in range(2)]
        a[t] = rows[:2]
        if ahead < count:
            a[ahead] = ahead_rows
    return tuple(jnp.concatenate([block[q] for block in a], 0) for q in range(2))


def stacked(re, im):
    return jnp.concatenate(
        [jnp.concatenate([re, im], 1), jnp.concatenate([-im, re], 1)], 0
    )


def times(left_re, left_im, right_re, right_im):
    return dot(jnp.concatenate([left_re, left_im], 1), stacked(right_re, right_im))


def halves_times(halves, right_re, right_im):
    half = right_re.shape[0] // 2
    top = jnp.concatenate([right_re, right_im], 1)
    low = jnp.concatenate([-right_im, right_re], 1)
    return dot(
        jnp.concatenate(halves, 1),
        jnp.concatenate([top[:half], low[:half], top[half:], low[half:]], 0),
    )


def vmem(count):
    return [pl.BlockSpec(memory_space=pltpu.VMEM)] * count


SMEM = pl.BlockSpec(memory_space=pltpu.SMEM)


def first_kernel(energy_ref, broadening_ref, onsite_ref, contact_ref, diag_ref, inv_ref):
    size = onsite_ref.shape[-1]
    re, im, kr, ki = onsite_ref[0, 0], onsite_ref[0, 1], contact_ref[0], contact_ref[1]
    krt, kit = kr.T, ki.T
    gamma = times(kr, ki, krt, -kit)
    row = lax.broadcasted_iota(jnp.int32, (size, size), 0)
    col = lax.broadcasted_iota(jnp.int32, (size, size), 1)
    unit = (row == col).astype(F32)
    diag_re = energy_ref[0] * unit - 0.5 * (re + re.T) - 0.5 * gamma[:, size:]
    diag_im = broadening_ref[0] * unit - 0.5 * (im - im.T) + 0.5 * gamma[:, :size]
    diag_ref[0], diag_ref[1] = diag_re, diag_im
    inv_ref[0], inv_ref[1] = inverse(diag_re, diag_im)


def is_odd(level):
    return ((lax.axis_index("transpor") >> level) & 1) == 1


def solve_into(inv, left_re, left_im, right_re, right_im, solved_refs, level):
    size = left_re.shape[-1]
    left = halves_times(inv, left_re, left_im)
    right = halves_times(inv, right_re, right_im)
    if len(solved_refs) == 1:
        (solved_ref,) = solved_refs
        solved_ref[0], solved_ref[1] = left[:, :size], left[:, size:]
        solved_ref[2], solved_ref[3] = right[:, :size], right[:, size:]
    else:
        odd = is_odd(level)
        early, late = jnp.where(odd, left, right), jnp.where(odd, right, left)
        for ref, value in zip(solved_refs, (early, late)):
            ref[0], ref[1] = value[:, :size], value[:, size:]


def start_kernel(inv_ref, behind_ref, coupling_ref, source_ref, left_ref, right_ref, *solved_refs):
    place, count = lax.axis_index("transpor"), lax.axis_size("transpor")
    left_re = jnp.where(place == 0, source_ref[0], -behind_ref[0, 0].T)
    left_im = jnp.where(place == 0, source_ref[1], behind_ref[0, 1].T)
    right_re = jnp.where(place == count - 1, 0.0, -coupling_ref[0, 0])
    right_im = jnp.where(place == count - 1, 0.0, -coupling_ref[0, 1])
    left_ref[0], left_ref[1] = left_re, left_im
    right_ref[0], right_ref[1] = right_re, right_im
    solve_into((inv_ref[0], inv_ref[1]), left_re, left_im, right_re, right_im, solved_refs, 0)


def has_left(level):
    return lax.axis_index("transpor") >= (1 << level)


def either(odd, one, other):
    return [jnp.where(odd, one[k], other[k]) for k in range(2)]


def reduced_diag(level, diag_ref, left_ref, right_ref, across_left, across_right):
    size = diag_ref.shape[-1]
    across_left = [jnp.where(has_left(level), part, 0.0) for part in across_left]
    change = times(left_ref[0], left_ref[1], *across_left) + times(
        right_ref[0], right_ref[1], *across_right
    )
    return diag_ref[0] - change[:, :size], diag_ref[1] - change[:, size:]


def next_couplings(level, left_ref, right_ref, beyond_left, beyond_right):
    size = left_ref.shape[-1]
    made = times(left_ref[0], left_ref[1], *beyond_left)
    left_re = jnp.where(has_left(level), -made[:, :size], left_ref[0])
    left_im = jnp.where(has_left(level), -made[:, size:], left_ref[1])
    made = times(right_ref[0], right_ref[1], *beyond_right)
    return left_re, left_im, -made[:, :size], -made[:, size:]


def level_kernel(
    level,
    diag_ref,
    left_ref,
    right_ref,
    near_ref,
    far_ref,
    diag_out_ref,
    left_out_ref,
    right_out_ref,
    *solved_refs,
):
    odd = is_odd(level)
    near, far = near_ref, far_ref
    across_left = either(odd, near[2:], far[2:])
    across_right = either(odd, far[:2], near[:2])
    re, im = reduced_diag(level, diag_ref, left_ref, right_ref, across_left, across_right)
    diag_out_ref[0], diag_out_ref[1] = re, im
    beyond_left = either(odd, near[:2], far[:2])
    beyond_right = either(odd, far[2:], near[2:])
    blocks = next_couplings(level, left_ref, right_ref, beyond_left, beyond_right)
    left_out_ref[0], left_out_ref[1], right_out_ref[0], right_out_ref[1] = blocks
    solve_into(inverse(re, im), *blocks, solved_refs, level + 1)


def invert_kernel(
    level, diag_ref, left_ref, right_ref, near_ref, far_ref, diag_out_ref, inv_ref
):
    odd = is_odd(level)
    across_left = either(odd, near_ref, far_ref)
    across_right = either(odd, far_ref, near_ref)
    re, im = reduced_diag(level, diag_ref, left_ref, right_ref, across_left, across_right)
    diag_out_ref[0], diag_out_ref[1] = re, im
    inv_ref[0], inv_ref[1] = inverse(re, im)


def couple_kernel(
    level,
    inv_ref,
    left_ref,
    right_ref,
    near_ref,
    far_ref,
    left_out_ref,
    right_out_ref,
    *solved_refs,
):
    odd = is_odd(level)
    beyond_left = either(odd, near_ref, far_ref)
    beyond_right = either(odd, far_ref, near_ref)
    blocks = next_couplings(level, left_ref, right_ref, beyond_left, beyond_right)
    left_out_ref[0], left_out_ref[1], right_out_ref[0], right_out_ref[1] = blocks
    solve_into((inv_ref[0], inv_ref[1]), *blocks, solved_refs, level + 1)


def link_change(level, left_ref, right_ref, near_ref):
    reached = has_left(level)
    link = [jnp.where(reached, left_ref[k], right_ref[k]) for k in range(2)]
    if near_ref.shape[0] == 2:
        return times(*link, near_ref[0], near_ref[1])
    return times(*link, *(jnp.where(reached, near_ref[k + 2], near_ref[k]) for k in range(2)))


def finish(level, inv, left_ref, near_ref, out_ref):
    size = left_ref.shape[-1]
    made = times(left_ref[0], left_ref[1], near_ref[0], near_ref[1])
    rhs_re = jnp.where(has_left(level), -made[:, :size], left_ref[0])
    rhs_im = jnp.where(has_left(level), -made[:, size:], left_ref[1])
    x = halves_times(inv, rhs_re, rhs_im)
    square = x * x
    both = square[:, :size] + square[:, size:]
    total = lax.dot_general(
        jnp.ones((8, size), F32),
        both,
        (((1,), (1,)), ((), ())),
        precision=HIGHEST,
        preferred_element_type=F32,
    )
    out_ref[...] = total


def last_kernel(level, diag_ref, left_ref, right_ref, near_ref, out_ref):
    size = diag_ref.shape[-1]
    change = link_change(level, left_ref, right_ref, near_ref)
    inv = inverse(diag_ref[0] - change[:, :size], diag_ref[1] - change[:, size:])
    finish(level, inv, left_ref, near_ref, out_ref)


def last_invert_kernel(level, diag_ref, left_ref, right_ref, near_ref, inv_ref):
    size = diag_ref.shape[-1]
    change = link_change(level, left_ref, right_ref, near_ref)
    inv_ref[0], inv_ref[1] = inverse(
        diag_ref[0] - change[:, :size], diag_ref[1] - change[:, size:]
    )


def last_solve_kernel(level, inv_ref, left_ref, near_ref, out_ref):
    finish(level, (inv_ref[0], inv_ref[1]), left_ref, near_ref, out_ref)


def call(kernel, outs, specs, flops=0):
    return pl.pallas_call(
        kernel,
        out_shape=outs,
        in_specs=specs,
        out_specs=jax.tree.map(lambda _: pl.BlockSpec(memory_space=pltpu.VMEM), outs),
        compiler_params=pltpu.CompilerParams(vmem_limit_bytes=16 << 20),
        cost_estimate=pl.CostEstimate(flops=flops, bytes_accessed=1 << 20, transcendentals=0),
    )


def summed_over(value, axis):
    parts = lax.all_to_all(value, axis, 0, 0, tiled=True)
    return jnp.sum(parts, axis=0, keepdims=True)


def local(onsite, coupling, source_coupling, energy, broadening, weights):
    size = onsite.shape[2]
    devices = lax.axis_size("transpor")
    levels = devices.bit_length() - 1
    block = jax.ShapeDtypeStruct((2, size, size), F32)
    pair = jax.ShapeDtypeStruct((4, size, size), F32)
    behind = lax.ppermute(
        coupling, "transpor", [(s, (s + 1) % devices) for s in range(devices)]
    )
    position = lax.axis_index("transpor")
    contact = jnp.where(
        position == 0, source_coupling, jnp.where(position == devices - 1, coupling[0], 0.0)
    )

    def solved_at(level):
        return [block, block] if level in SPLIT_LEVELS else [pair]

    diag, inv = call(first_kernel, [block] * 2, [SMEM, SMEM] + vmem(2), 4 << 30)(
        energy, broadening, onsite, contact
    )
    left, right, *solved = call(start_kernel, [block, block] + solved_at(0), vmem(4))(
        inv, behind, coupling, source_coupling
    )
    for level in range(levels - 1):
        distance = 1 << level
        to_near = [(s, s ^ distance) for s in range(devices)]
        to_far = [
            (s, (s + (distance if s & distance else -distance)) % devices) for s in range(devices)
        ]
        near = lax.ppermute(solved[0], "transpor", to_near)
        far = lax.ppermute(solved[-1], "transpor", to_far)
        outs = [block, block] + solved_at(level + 1)
        if level in SPLIT_LEVELS:
            early = solved[0]
            if level == 2:
                near, early = lax.optimization_barrier((near, solved[0]))
            late_near = lax.ppermute(solved[1], "transpor", to_near)
            late_far = lax.ppermute(early, "transpor", to_far)
            diag, inv = call(
                functools.partial(invert_kernel, level), [block, block], vmem(5), 4 << 30
            )(diag, left, right, near, far)
            left, right, *solved = call(functools.partial(couple_kernel, level), outs, vmem(5))(
                inv, left, right, late_near, late_far
            )
        else:
            diag, left, right, *solved = call(
                functools.partial(level_kernel, level), [block] + outs, vmem(5), 4 << 30
            )(diag, left, right, near, far)
    level = levels - 1
    to_near = [(s, s ^ (1 << level)) for s in range(devices)]
    near = lax.ppermute(solved[0], "transpor", to_near)
    count = lax.axis_size("energy")
    result = jax.ShapeDtypeStruct((8, size), F32)
    if level in SPLIT_LEVELS:
        late_near = lax.ppermute(solved[1], "transpor", to_near)
        inv = call(functools.partial(last_invert_kernel, level), block, vmem(4), 4 << 30)(
            diag, left, right, near
        )
        row = call(functools.partial(last_solve_kernel, level), result, vmem(3))(
            inv, left, late_near
        )
    else:
        row = call(functools.partial(last_kernel, level), result, vmem(4))(
            diag, left, right, near
        )
    weighted = weights[0] * row[0]
    return summed_over(weighted.reshape(count, size // count), "energy")


def solution(mesh):
    placed = (
        P("transpor", None, None, None),
        P("transpor", None, None, None),
        P(),
        P("energy"),
        P("energy"),
        P("energy"),
    )
    return jax.shard_map(
        local, mesh=mesh, in_specs=placed, out_specs=P("transpor", "energy"), check_vma=False
    )
```

```python
import functools

import jax
import jax.numpy as jnp
from jax import lax
from jax.experimental import pallas as pl
from jax.experimental.pallas import tpu as pltpu
from jax.sharding import PartitionSpec as P

F32 = jnp.float32
BF16 = jnp.bfloat16
HIGHEST = lax.Precision.HIGHEST
ROWS = 8
SPLIT_LEVELS = (0, 1, 2, 3, 4)


def dot(left, right):
    return jnp.dot(left, right, precision=HIGHEST, preferred_element_type=F32)


def row_of(value, k):
    return jnp.broadcast_to(value[k : k + 1, :], value.shape)


def column_of(value, j):
    index = jnp.full(value.shape, j, jnp.int32)
    return jnp.take_along_axis(value, index, axis=1, mode="promise_in_bounds")


def tree_sum(terms):
    terms = list(terms)
    while len(terms) > 1:
        paired = [terms[i] + terms[i + 1] for i in range(0, len(terms) - 1, 2)]
        terms = paired + terms[len(terms) - len(terms) % 2 :]
    return terms[0]


def mul(a, b):
    return a[0] * b[0] - a[1] * b[1], a[0] * b[1] + a[1] * b[0]


def mul_conj(a, b):
    return a[0] * b[0] + a[1] * b[1], a[1] * b[0] - a[0] * b[1]


def add(a, b):
    return a[0] + b[0], a[1] + b[1]


def sub(a, b):
    return a[0] - b[0], a[1] - b[1]


def chosen(where, a, b):
    return jnp.where(where, a[0], b[0]), jnp.where(where, a[1], b[1])


def eliminate_panel(columns, rows, place):
    columns, rows = list(columns), list(rows)
    zero = (0.0, 0.0)
    same = cross = None
    for k in range(0, ROWS, 2):
        x, y = columns[k], columns[k + 1]
        a, c = [tuple(row_of(part, k + r) for part in x) for r in range(2)]
        b, d = [tuple(row_of(part, k + r) for part in y) for r in range(2)]
        det = sub(mul(a, d), mul(b, c))
        inv = 1.0 / (det[0] * det[0] + det[1] * det[1])
        first, here = place == k, (place == k) | (place == k + 1)
        x, y = chosen(here, zero, x), chosen(here, zero, y)
        t0 = mul_conj(sub(mul(x, d), mul(y, c)), det)
        t1 = mul_conj(sub(mul(y, a), mul(x, b)), det)
        u0, u1 = (t0[0] * inv, t0[1] * inv), (t1[0] * inv, t1[1] * inv)
        for j in range(k + 2, ROWS):
            r0, r1 = [tuple(row_of(part, k + r) for part in columns[j]) for r in range(2)]
            if j < k + 4:
                w = add(mul(t0, r0), mul(t1, r1))
                columns[j] = sub(columns[j], (inv * w[0], inv * w[1]))
            else:
                columns[j] = sub(columns[j], add(mul(u0, r0), mul(u1, r1)))
        r0, r1 = [[row_of(part, k + r) for part in rows] for r in range(2)]
        taken = [
            (u0[0] * r0[q] + u0[1] * r0[q + 2]) + (u1[0] * r1[q] + u1[1] * r1[q + 2])
            for q in range(2)
        ] + [
            (u0[0] * r0[q + 2] - u0[1] * r0[q]) + (u1[0] * r1[q + 2] - u1[1] * r1[q])
            for q in range(2)
        ]
        rows = [part - change for part, change in zip(rows, taken)]
        scale = (det[0] * inv, -(det[1] * inv))
        p, q = mul(chosen(first, d, a), scale), mul(chosen(first, b, c), scale)
        same = p if k == 0 else chosen(here, p, same)
        cross = q if k == 0 else chosen(here, q, cross)
    odd = (place & 1) == 1
    other = [
        jnp.where(odd, pltpu.roll(part, 1, 0), pltpu.roll(part, ROWS - 1, 0)) for part in rows
    ]
    return [
        (same[0] * rows[q] + same[1] * rows[q + 2])
        - (cross[0] * other[q] + cross[1] * other[q + 2])
        for q in range(2)
    ] + [
        (same[0] * rows[q + 2] - same[1] * rows[q])
        - (cross[0] * other[q + 2] - cross[1] * other[q])
        for q in range(2)
    ]


def three_parts(value):
    high = value.astype(BF16)
    rest = value - high.astype(F32)
    middle = rest.astype(BF16)
    return high, middle, (rest - middle.astype(F32)).astype(BF16)


def short_dot(left, right):
    (l0, l1, l2), (r0, r1, r2) = left, right
    total = None
    for one, other, low, high in ((l2, l1, r0, r1), (l1, l0, r0, r2), (l0, l0, r1, r0)):
        part = jnp.dot(
            jnp.concatenate([one, other], 1),
            jnp.concatenate([low, high], 0),
            preferred_element_type=F32,
        )
        total = part if total is None else total + part
    return total


def inverse(re, im):
    size = re.shape[0]
    half = size // 2
    count = size // ROWS
    low = lax.broadcasted_iota(jnp.int32, (size, size), 1) < half
    halves = (
        jnp.where(low, re, pltpu.roll(im, half, 1)),
        jnp.where(low, pltpu.roll(re, half, 1), im),
    )
    a = [[part[ROWS * b : ROWS * (b + 1)] for part in halves] for b in range(count)]
    place = lax.broadcasted_iota(jnp.int32, (ROWS, size), 0)
    lane = lax.broadcasted_iota(jnp.int32, (ROWS, size), 1)
    empty = jnp.zeros((ROWS, 2 * size), F32)

    def gap(groups):
        return [jnp.zeros((2 * ROWS * groups, 2 * size), BF16)] if groups else []

    def times_i(part):
        turned = pltpu.roll(part, half, 1)
        return jnp.where(lane < half, -turned, turned)

    for t in range(count):
        side, base = divmod(ROWS * t, half)
        inside = (lane & (half - 1)) - base
        pivots = (inside >= 0) & (inside < ROWS)

        def cleared(block, q):
            return jnp.where(pivots, 0.0, a[block][q]) if q == side else a[block][q]

        def pivot_columns(block):
            part = a[block][side]
            return [
                (column_of(part, base + j), column_of(part, half + base + j)) for j in range(ROWS)
            ]

        rows = list(a[t]) + [times_i(part) for part in a[t]]
        rows[side] = jnp.where(pivots, (lane - base == place).astype(F32), rows[side])
        rows[side + 2] = jnp.where(
            pivots, (lane - half - base == place).astype(F32), rows[side + 2]
        )
        rows = eliminate_panel(pivot_columns(t), rows, place)
        ahead = t + 1
        if ahead < count:
            factors = pivot_columns(ahead)
            spread = [[row_of(part, j) for part in rows] for j in range(ROWS)]
            ahead_rows = [
                cleared(ahead, q)
                - tree_sum(
                    m[0] * row[q] + m[1] * row[q + 2] for m, row in zip(factors, spread)
                )
                for q in range(2)
            ]
        others = [b for b in range(count) if ahead == count or b not in (t, ahead)]
        left = three_parts(jnp.concatenate([a[b][side] for b in others], 0))
        group, second = divmod(base // ROWS, 2)
        groups = half // (2 * ROWS)
        right = []
        tops, lows = [
            three_parts(jnp.concatenate([empty, part] if second else [part, empty], 0))
            for part in (jnp.concatenate(rows[:2], 1), jnp.concatenate(rows[2:], 1))
        ]
        for top, bottom in zip(tops, lows):
            right.append(
                jnp.concatenate(
                    gap(group) + [top] + gap(groups - 1) + [bottom] + gap(groups - 1 - group), 0
                )
            )
        change = short_dot(left, right)
        for x, b in enumerate(others):
            part = change[ROWS * x : ROWS * (x + 1)]
            a[b] = [cleared(b, q) - part[:, q * size : (q + 1) * size] for q in range(2)]
        a[t] = rows[:2]
        if ahead < count:
            a[ahead] = ahead_rows
    return tuple(jnp.concatenate([block[q] for block in a], 0) for q in range(2))


def stacked(re, im):
    return jnp.concatenate(
        [jnp.concatenate([re, im], 1), jnp.concatenate([-im, re], 1)], 0
    )


def times(left_re, left_im, right_re, right_im):
    return dot(jnp.concatenate([left_re, left_im], 1), stacked(right_re, right_im))


def halves_times(halves, right_re, right_im):
    half = right_re.shape[0] // 2
    top = jnp.concatenate([right_re, right_im], 1)
    low = jnp.concatenate([-right_im, right_re], 1)
    return dot(
        jnp.concatenate(halves, 1),
        jnp.concatenate([top[:half], low[:half], top[half:], low[half:]], 0),
    )


def vmem(count):
    return [pl.BlockSpec(memory_space=pltpu.VMEM)] * count


SMEM = pl.BlockSpec(memory_space=pltpu.SMEM)


def first_kernel(energy_ref, broadening_ref, onsite_ref, contact_ref, diag_ref, inv_ref):
    size = onsite_ref.shape[-1]
    re, im, kr, ki = onsite_ref[0, 0], onsite_ref[0, 1], contact_ref[0], contact_ref[1]
    krt, kit = kr.T, ki.T
    gamma = times(kr, ki, krt, -kit)
    row = lax.broadcasted_iota(jnp.int32, (size, size), 0)
    col = lax.broadcasted_iota(jnp.int32, (size, size), 1)
    unit = (row == col).astype(F32)
    diag_re = energy_ref[0] * unit - 0.5 * (re + re.T) - 0.5 * gamma[:, size:]
    diag_im = broadening_ref[0] * unit - 0.5 * (im - im.T) + 0.5 * gamma[:, :size]
    diag_ref[0], diag_ref[1] = diag_re, diag_im
    inv_ref[0], inv_ref[1] = inverse(diag_re, diag_im)


def is_odd(level):
    return ((lax.axis_index("transpor") >> level) & 1) == 1


def solve_into(inv, left_re, left_im, right_re, right_im, solved_refs, level):
    size = left_re.shape[-1]
    left = halves_times(inv, left_re, left_im)
    right = halves_times(inv, right_re, right_im)
    if len(solved_refs) == 1:
        (solved_ref,) = solved_refs
        solved_ref[0], solved_ref[1] = left[:, :size], left[:, size:]
        solved_ref[2], solved_ref[3] = right[:, :size], right[:, size:]
    else:
        odd = is_odd(level)
        early, late = jnp.where(odd, left, right), jnp.where(odd, right, left)
        for ref, value in zip(solved_refs, (early, late)):
            ref[0], ref[1] = value[:, :size], value[:, size:]


def start_kernel(inv_ref, behind_ref, coupling_ref, source_ref, left_ref, right_ref, *solved_refs):
    place, count = lax.axis_index("transpor"), lax.axis_size("transpor")
    left_re = jnp.where(place == 0, source_ref[0], -behind_ref[0, 0].T)
    left_im = jnp.where(place == 0, source_ref[1], behind_ref[0, 1].T)
    right_re = jnp.where(place == count - 1, 0.0, -coupling_ref[0, 0])
    right_im = jnp.where(place == count - 1, 0.0, -coupling_ref[0, 1])
    left_ref[0], left_ref[1] = left_re, left_im
    right_ref[0], right_ref[1] = right_re, right_im
    solve_into((inv_ref[0], inv_ref[1]), left_re, left_im, right_re, right_im, solved_refs, 0)


def has_left(level):
    return lax.axis_index("transpor") >= (1 << level)


def either(odd, one, other):
    return [jnp.where(odd, one[k], other[k]) for k in range(2)]


def reduced_diag(level, diag_ref, left_ref, right_ref, across_left, across_right):
    size = diag_ref.shape[-1]
    across_left = [jnp.where(has_left(level), part, 0.0) for part in across_left]
    change = times(left_ref[0], left_ref[1], *across_left) + times(
        right_ref[0], right_ref[1], *across_right
    )
    return diag_ref[0] - change[:, :size], diag_ref[1] - change[:, size:]


def next_couplings(level, left_ref, right_ref, beyond_left, beyond_right):
    size = left_ref.shape[-1]
    made = times(left_ref[0], left_ref[1], *beyond_left)
    left_re = jnp.where(has_left(level), -made[:, :size], left_ref[0])
    left_im = jnp.where(has_left(level), -made[:, size:], left_ref[1])
    made = times(right_ref[0], right_ref[1], *beyond_right)
    return left_re, left_im, -made[:, :size], -made[:, size:]


def level_kernel(
    level,
    diag_ref,
    left_ref,
    right_ref,
    near_ref,
    far_ref,
    diag_out_ref,
    left_out_ref,
    right_out_ref,
    *solved_refs,
):
    odd = is_odd(level)
    near, far = near_ref, far_ref
    across_left = either(odd, near[2:], far[2:])
    across_right = either(odd, far[:2], near[:2])
    re, im = reduced_diag(level, diag_ref, left_ref, right_ref, across_left, across_right)
    diag_out_ref[0], diag_out_ref[1] = re, im
    beyond_left = either(odd, near[:2], far[:2])
    beyond_right = either(odd, far[2:], near[2:])
    blocks = next_couplings(level, left_ref, right_ref, beyond_left, beyond_right)
    left_out_ref[0], left_out_ref[1], right_out_ref[0], right_out_ref[1] = blocks
    solve_into(inverse(re, im), *blocks, solved_refs, level + 1)


def near_kernel(level, diag_ref, left_ref, right_ref, near_ref, out_ref):
    size = diag_ref.shape[-1]
    link = either(is_odd(level), left_ref, right_ref)
    change = times(*link, near_ref[0], near_ref[1])
    out_ref[0], out_ref[1] = diag_ref[0] - change[:, :size], diag_ref[1] - change[:, size:]


def invert_kernel(level, diag_ref, left_ref, right_ref, far_ref, diag_out_ref, inv_ref):
    size = diag_ref.shape[-1]
    odd = is_odd(level)
    link = either(odd, right_ref, left_ref)
    there = odd | has_left(level)
    far = [jnp.where(there, far_ref[k], 0.0) for k in range(2)]
    change = times(*link, *far)
    re, im = diag_ref[0] - change[:, :size], diag_ref[1] - change[:, size:]
    diag_out_ref[0], diag_out_ref[1] = re, im
    inv_ref[0], inv_ref[1] = inverse(re, im)


def couple_kernel(
    level,
    inv_ref,
    left_ref,
    right_ref,
    near_ref,
    far_ref,
    left_out_ref,
    right_out_ref,
    *solved_refs,
):
    odd = is_odd(level)
    beyond_left = either(odd, near_ref, far_ref)
    beyond_right = either(odd, far_ref, near_ref)
    blocks = next_couplings(level, left_ref, right_ref, beyond_left, beyond_right)
    left_out_ref[0], left_out_ref[1], right_out_ref[0], right_out_ref[1] = blocks
    solve_into((inv_ref[0], inv_ref[1]), *blocks, solved_refs, level + 1)


def link_change(level, left_ref, right_ref, near_ref):
    reached = has_left(level)
    link = [jnp.where(reached, left_ref[k], right_ref[k]) for k in range(2)]
    if near_ref.shape[0] == 2:
        return times(*link, near_ref[0], near_ref[1])
    return times(*link, *(jnp.where(reached, near_ref[k + 2], near_ref[k]) for k in range(2)))


def finish(level, inv, left_ref, near_ref, out_ref):
    size = left_ref.shape[-1]
    made = times(left_ref[0], left_ref[1], near_ref[0], near_ref[1])
    rhs_re = jnp.where(has_left(level), -made[:, :size], left_ref[0])
    rhs_im = jnp.where(has_left(level), -made[:, size:], left_ref[1])
    x = halves_times(inv, rhs_re, rhs_im)
    square = x * x
    both = square[:, :size] + square[:, size:]
    total = lax.dot_general(
        jnp.ones((8, size), F32),
        both,
        (((1,), (1,)), ((), ())),
        precision=HIGHEST,
        preferred_element_type=F32,
    )
    out_ref[...] = total


def last_kernel(level, diag_ref, left_ref, right_ref, near_ref, out_ref):
    size = diag_ref.shape[-1]
    change = link_change(level, left_ref, right_ref, near_ref)
    inv = inverse(diag_ref[0] - change[:, :size], diag_ref[1] - change[:, size:])
    finish(level, inv, left_ref, near_ref, out_ref)


def last_invert_kernel(level, diag_ref, left_ref, right_ref, near_ref, inv_ref):
    size = diag_ref.shape[-1]
    change = link_change(level, left_ref, right_ref, near_ref)
    inv_ref[0], inv_ref[1] = inverse(
        diag_ref[0] - change[:, :size], diag_ref[1] - change[:, size:]
    )


def last_solve_kernel(level, inv_ref, left_ref, near_ref, out_ref):
    finish(level, (inv_ref[0], inv_ref[1]), left_ref, near_ref, out_ref)


def call(kernel, outs, specs, flops=0):
    return pl.pallas_call(
        kernel,
        out_shape=outs,
        in_specs=specs,
        out_specs=jax.tree.map(lambda _: pl.BlockSpec(memory_space=pltpu.VMEM), outs),
        compiler_params=pltpu.CompilerParams(vmem_limit_bytes=16 << 20),
        cost_estimate=pl.CostEstimate(flops=flops, bytes_accessed=1 << 20, transcendentals=0),
    )


def summed_over(value, axis):
    parts = lax.all_to_all(value, axis, 0, 0, tiled=True)
    return jnp.sum(parts, axis=0, keepdims=True)


def local(onsite, coupling, source_coupling, energy, broadening, weights):
    size = onsite.shape[2]
    devices = lax.axis_size("transpor")
    levels = devices.bit_length() - 1
    block = jax.ShapeDtypeStruct((2, size, size), F32)
    pair = jax.ShapeDtypeStruct((4, size, size), F32)
    behind = lax.ppermute(
        coupling, "transpor", [(s, (s + 1) % devices) for s in range(devices)]
    )
    position = lax.axis_index("transpor")
    contact = jnp.where(
        position == 0, source_coupling, jnp.where(position == devices - 1, coupling[0], 0.0)
    )

    def solved_at(level):
        return [block, block] if level in SPLIT_LEVELS else [pair]

    diag, inv = call(first_kernel, [block] * 2, [SMEM, SMEM] + vmem(2), 4 << 30)(
        energy, broadening, onsite, contact
    )
    left, right, *solved = call(start_kernel, [block, block] + solved_at(0), vmem(4))(
        inv, behind, coupling, source_coupling
    )
    for level in range(levels - 1):
        distance = 1 << level
        to_near = [(s, s ^ distance) for s in range(devices)]
        to_far = [
            (s, (s + (distance if s & distance else -distance)) % devices) for s in range(devices)
        ]
        near = lax.ppermute(solved[0], "transpor", to_near)
        far = lax.ppermute(solved[-1], "transpor", to_far)
        outs = [block, block] + solved_at(level + 1)
        if level in SPLIT_LEVELS:
            early = solved[0]
            if level == 2:
                near, early = lax.optimization_barrier((near, solved[0]))
            late_near = lax.ppermute(solved[1], "transpor", to_near)
            late_far = lax.ppermute(early, "transpor", to_far)
            diag = call(functools.partial(near_kernel, level), block, vmem(4))(
                diag, left, right, near
            )
            diag, inv = call(
                functools.partial(invert_kernel, level), [block, block], vmem(4), 4 << 30
            )(diag, left, right, far)
            left, right, *solved = call(functools.partial(couple_kernel, level), outs, vmem(5))(
                inv, left, right, late_near, late_far
            )
        else:
            diag, left, right, *solved = call(
                functools.partial(level_kernel, level), [block] + outs, vmem(5), 4 << 30
            )(diag, left, right, near, far)
    level = levels - 1
    to_near = [(s, s ^ (1 << level)) for s in range(devices)]
    near = lax.ppermute(solved[0], "transpor", to_near)
    count = lax.axis_size("energy")
    result = jax.ShapeDtypeStruct((8, size), F32)
    if level in SPLIT_LEVELS:
        late_near = lax.ppermute(solved[1], "transpor", to_near)
        inv = call(functools.partial(last_invert_kernel, level), block, vmem(4), 4 << 30)(
            diag, left, right, near
        )
        row = call(functools.partial(last_solve_kernel, level), result, vmem(3))(
            inv, left, late_near
        )
    else:
        row = call(functools.partial(last_kernel, level), result, vmem(4))(
            diag, left, right, near
        )
    weighted = weights[0] * row[0]
    return summed_over(weighted.reshape(count, size // count), "energy")


def solution(mesh):
    placed = (
        P("transpor", None, None, None),
        P("transpor", None, None, None),
        P(),
        P("energy"),
        P("energy"),
        P("energy"),
    )
    return jax.shard_map(
        local, mesh=mesh, in_specs=placed, out_specs=P("transpor", "energy"), check_vma=False
    )
```
